256 devices in a mesh: replica: 8 (over y_lo, x), fsdp: 32 (over y_hi, z, core).
Axes of the slice: x: 4, y: 4 (y_hi: 2, y_lo: 2; y = y_hi * 2 + y_lo), z: 8, core: 2. Of those that a mesh axis runs over, the one named last changes fastest.
Arguments:
- hidden: bfloat16 [8, 4096, 8192], P('replica', 'fsdp'), may hold values from -6 to 6
- norm_gain: bfloat16 [8, 8192], P('replica', 'fsdp'), may hold values from 0.099609375 to 1.8984375
- key_value_weight: bfloat16 [8, 8192, 1024], P('replica', 'fsdp'), may hold values from -0.0625 to 0.0625
- upstream: bfloat16 [8, 4096, 1024], P('replica', 'fsdp'), may hold values from -6 to 6
- global_weight: float32 [8192, 1024], P('fsdp'), may hold values from -6 to 6
- global_momentum: float32 [8192, 1024], P('fsdp'), may hold values from -6 to 6
- replica_delta: float32 [8, 8192, 1024], P('replica', 'fsdp'), may hold values from -6 to 6
Outputs:
- keys_values: bfloat16 [8, 4096, 1024], P('replica', 'fsdp')
- input_gradient: bfloat16 [8, 4096, 8192], P('replica', 'fsdp')
- weight_gradient: bfloat16 [8, 8192, 1024], P('replica', 'fsdp')
- gain_gradient: bfloat16 [8, 8192], P('replica', 'fsdp')
- merged_weight: float32 [8192, 1024], P('fsdp')
- merged_momentum: float32 [8192, 1024], P('fsdp')
The draws below stay inside these ranges and needn't reach their ends.
All inputs are finite; a program needn't handle non-finite values.
Results may differ from the reference program's by a relative error of at most 0.007.
Values may be sent and summed in bfloat16 or wider, within the bound.
A program may use at most 192 MiB of HBM per device.

```python
import jax
import jax.numpy as jnp
from jax import lax

D = 8192
KV_WIDTH = 1024
TOKENS = 4096
N_REPLICA = 8


def levels(own_key, shape, split, low, top_value):
    def one(position, parts):
        heights = jax.random.uniform(jax.random.fold_in(jax.random.fold_in(own_key, 6), position), (parts,), jnp.float32, low / len(split), top_value / len(split))
        return jnp.repeat(jnp.exp(heights), shape[position] // parts).reshape((-1,) + (1,) * (len(shape) - position - 1))

    loudness = one(*split[0])
    for cut in split[1:]:
        loudness = loudness * one(*cut)
    return loudness


def scatter_about(stream_key, dims, spread, bound, shards=(), dtype=jnp.bfloat16):
    factor_of = levels(stream_key, dims, shards, -0.22, 0.18) if shards else 1.0
    values = jax.random.normal(stream_key, dims, jnp.float32) * spread * factor_of
    return jnp.minimum(jnp.maximum(values, -bound), bound).astype(dtype)


def setup_inputs(seed: int = 0) -> dict:
    arg_keys = jax.random.split(jax.random.key(seed), 8)
    return {
        "hidden": scatter_about(arg_keys[0], (N_REPLICA, TOKENS, D), 1.0, 6.0, ((0, 8), (1, 32))),
        "norm_gain": jnp.clip(1.0 + 0.18 * jax.random.normal(arg_keys[1], (N_REPLICA, D), jnp.float32), 0.099609375, 1.8984375).astype(jnp.bfloat16),
        "key_value_weight": scatter_about(arg_keys[2], (N_REPLICA, D, KV_WIDTH), D ** -0.5, 0.0625, ((0, 8), (1, 32))),
        "upstream": scatter_about(arg_keys[3], (N_REPLICA, TOKENS, KV_WIDTH), 1.0, 6.0, ((0, 8), (1, 32))),
        "global_weight": scatter_about(arg_keys[4], (D, KV_WIDTH), 1.0, 6.0, ((0, 32),), jnp.float32),
        "global_momentum": scatter_about(arg_keys[5], (D, KV_WIDTH), 1.0, 6.0, ((0, 32),), jnp.float32),
        "replica_delta": scatter_about(arg_keys[6], (N_REPLICA, D, KV_WIDTH), 1.0, 6.0, ((0, 8), (1, 32)), jnp.float32),
    }


def one_replica(pieces):
    hidden, norm_gain, weight, upstream = pieces
    tokens = hidden.astype(jnp.float32)
    square_mean = lax.optimization_barrier(jnp.mean(tokens * tokens, axis=-1, keepdims=True))
    inverse = lax.rsqrt(square_mean + 1e-05)
    scaled = tokens * inverse
    gain_row = norm_gain.astype(jnp.float32)
    normed = (scaled * gain_row).astype(jnp.bfloat16)
    keys_values = jnp.dot(normed, weight, preferred_element_type=jnp.float32).astype(jnp.bfloat16)
    weight_gradient = lax.dot_general(normed, upstream, (((0,), (0,)), ((), ())), preferred_element_type=jnp.float32).astype(jnp.bfloat16)
    back = lax.dot_general(upstream, weight, (((1,), (1,)), ((), ())), preferred_element_type=jnp.float32)
    gain_gradient = lax.optimization_barrier(jnp.sum(back * scaled, axis=0)).astype(jnp.bfloat16)
    upper = back * gain_row
    inner = lax.optimization_barrier(jnp.mean(upper * scaled, axis=-1, keepdims=True))
    input_gradient = (inverse * (upper - scaled * inner)).astype(jnp.bfloat16)
    return (keys_values, input_gradient, weight_gradient, gain_gradient)

def reference(hidden, norm_gain, key_value_weight, upstream, global_weight, global_momentum, replica_delta):
    keys_values, input_gradient, weight_gradient, gain_gradient = lax.map(one_replica, (hidden, norm_gain, key_value_weight, upstream))
    average = lax.optimization_barrier(jnp.sum(replica_delta, axis=0)) / N_REPLICA
    merged_momentum = 0.9 * global_momentum + average
    merged_weight = global_weight - 0.7 * (average + 0.9 * merged_momentum)
    return (keys_values, input_gradient, weight_gradient, gain_gradient, merged_weight, merged_momentum)
```

```python
import functools

import jax
import jax.numpy as jnp
from jax import lax
from jax.experimental import pallas as pl
from jax.experimental.pallas import tpu as pltpu
from jax.sharding import PartitionSpec as P

MESH = pl.DeviceIdType.MESH
F32 = jnp.float32
BF16 = jnp.bfloat16
T = 128
F = 256
K = 1024
D = 8192
R = 64


def device(h, z, c, low, x):
    return {"replica": low * 4 + x, "fsdp": h * 16 + z * 2 + c}


def kernel(
    x_hbm, gain_ref, w_hbm, u_hbm, delta_hbm, gw_hbm, gm_hbm,
    kv_out, dx_out, dw_out, gg_out, mw_out, mm_out,
    xv, xq, wv, wq, uv, uall, ub, uh, inv, gcol, rs_out, rs_in,
    kvs, kvr, gps, gpr, dv, dbf, d1, d2s, d2r, davg, gwv, gmv, dxv, dwv, kvv,
    ld, lq, st, ag_s, ag_r, rs_s, rs_r, x_s, x_r, u_s, u_r, b_s, b_r, k_s, k_r, g_s, g_r,
    d1_s, d1_r, d2_s, d2_r, d3_s, d3_r,
):
    fsdp, rep = lax.axis_index("fsdp"), lax.axis_index("replica")
    h, z, c = fsdp // 16, (fsdp % 16) // 2, fsdp % 2
    low, xx = rep // 4, rep % 4

    def mate(k):
        return device((h + k // 2) % 2, z, (c + k % 2) % 2, low, xx)

    def along(step):
        return device(h, (z + 8 + step) % 8, c, low, xx)

    def column(k, j):
        at = ((h + k // 2) % 2) * 4096 + j * 512 + ((c + k % 2) % 2) * 256
        return pl.ds(pl.multiple_of(at, 256), 256)

    def remote(src, dst, s, r, to):
        return pltpu.make_async_remote_copy(
            src_ref=src, dst_ref=dst, send_sem=s, recv_sem=r, device_id=to, device_id_type=MESH
        )

    load_w = pltpu.make_async_copy(w_hbm, wv, ld.at[0])
    load_u = pltpu.make_async_copy(u_hbm, uv, ld.at[1])
    load_x = pltpu.make_async_copy(x_hbm, xv, ld.at[2])
    load_d = pltpu.make_async_copy(delta_hbm, dv, ld.at[3])
    load_gw = pltpu.make_async_copy(gw_hbm, gwv, ld.at[4])
    load_gm = pltpu.make_async_copy(gm_hbm, gmv, ld.at[5])
    load_w.start()
    load_x.start()
    load_u.start()
    load_d.start()

    def own_x(j):
        return pltpu.make_async_copy(x_hbm.at[:, column(0, j)], xq.at[j, pl.ds(0, T)], lq.at[j])

    barrier = pltpu.get_barrier_semaphore()
    others = [along(s) for s in range(1, 8)] + [mate(k) for k in range(1, 4)]
    others += [device(h, z, c, low, (xx + q) % 4) for q in range(1, 4)]
    others += [device(h, z, c, 1 - low, xx)]
    for to in others:
        pl.semaphore_signal(barrier, inc=1, device_id=to, device_id_type=MESH)

    gain_row = gain_ref[...].astype(F32)
    gcol[...] = jnp.transpose(jnp.broadcast_to(gain_row, (128, F)))
    load_w.wait()
    for half in range(2):
        rows = pl.ds(half * 128, 128)
        g = gcol[rows, :]
        for t in range(8):
            cols = pl.ds(t * 128, 128)
            wq[z, half, :, cols] = (wv[rows, cols].astype(F32) * g).astype(BF16)
    pl.semaphore_wait(barrier, len(others))

    chains = [(1, 0, 0), (-1, 1, 0), (1, 1, 1), (-1, 0, 1)]

    def gather(n, chain):
        sign, half, short = chain
        d = 0 if sign > 0 else 1
        block = wq.at[(z + 8 - sign * (n - 1)) % 8, half]
        return remote(block, block, ag_s.at[d, n - 1, half], ag_r.at[d, n - 1, half], along(sign))

    def gather_in(n, chain):
        sign, half, short = chain
        d = 0 if sign > 0 else 1
        block = wq.at[(z + 8 - sign * n) % 8, half]
        return remote(block, block, ag_s.at[d, n - 1, half], ag_r.at[d, n - 1, half], along(sign))

    for chain in chains:
        gather(1, chain).start()

    def x_copy(k, j):
        return remote(
            x_hbm.at[:, column(k, j)], xq.at[j, pl.ds(k * T, T)], x_s.at[k - 1, j], x_r.at[k - 1, j], mate(k)
        )

    @pl.loop(0, 8)
    def _(j):
        for k in (2, 3, 1):
            x_copy(k, j).start()
        own_x(j).start()

    def quarter(i):
        return pl.ds(pl.multiple_of(i * R, R), R)

    def d1_copy(q):
        to = (xx + q) % 4
        return remote(dbf.at[quarter(to)], d1.at[q - 1], d1_s.at[q - 1], d1_r.at[q - 1], device(h, z, c, low, to))

    load_d.wait()
    dbf[...] = dv[...].astype(BF16)
    for q in range(1, 4):
        d1_copy(q).start()

    load_x.wait()

    def squares(i, acc):
        v = xv[:, pl.ds(pl.multiple_of(i * 256, 256), 256)].astype(F32)
        return acc + v * v

    acc = lax.fori_loop(0, 32, squares, jnp.zeros((T, 256), F32))
    inverse = lax.rsqrt(jnp.sum(acc, axis=1, keepdims=True) * (1.0 / D) + 1e-05)
    inv[...] = jnp.broadcast_to(inverse, (T, 128))
    load_u.wait()
    uall[pl.ds(0, T), :] = (uv[...].astype(F32) * inverse).astype(BF16)

    def u_copy(k):
        return remote(uall.at[pl.ds(0, T)], uall.at[pl.ds(k * T, T)], u_s.at[k - 1], u_r.at[k - 1], mate(k))

    for k in (2, 3, 1):
        u_copy(k).start()
    load_gw.start()
    load_gm.start()

    def hop(n):
        for chain in chains:
            gather_in(n, chain).wait_recv()
            if n < 3 or chain[2] == 0:
                gather(n + 1, chain).start()

    hop(1)

    d2_copy = remote(d2s, d2r, d2_s, d2_r, device(h, z, c, 1 - low, xx))
    for q in range(1, 4):
        d1_copy(q).wait_recv()
    d2s[...] = (
        dv[quarter(xx), :] + d1[0].astype(F32) + d1[1].astype(F32) + d1[2].astype(F32)
    ).astype(BF16)
    d2_copy.start()

    hop(2)

    def d3_copy(q):
        block = davg.at[quarter(xx)]
        return remote(block, block, d3_s.at[q - 1], d3_r.at[q - 1], device(h, z, c, low, (xx + q) % 4))

    d2_copy.wait_recv()
    davg[quarter(xx), :] = ((d2s[...].astype(F32) + d2r[...].astype(F32)) * 0.125).astype(BF16)
    for q in range(1, 4):
        d3_copy(q).start()

    hop(3)

    def d3_in(q):
        block = davg.at[quarter((xx + 4 - q) % 4)]
        return remote(block, block, d3_s.at[q - 1], d3_r.at[q - 1], device(h, z, c, low, (xx + q) % 4))

    for q in range(1, 4):
        d3_in(q).wait_recv()
    load_gw.wait()
    load_gm.wait()

    @pl.loop(0, 8)
    def _(i):
        rows = pl.ds(pl.multiple_of(i * 32, 32), 32)
        average = davg[rows, :].astype(F32)
        fresh = 0.9 * gmv[rows, :] + average
        gmv[rows, :] = fresh
        gwv[rows, :] = gwv[rows, :] - 0.7 * (average + 0.9 * fresh)

    store_mw = pltpu.make_async_copy(gwv, mw_out, st.at[0])
    store_mm = pltpu.make_async_copy(gmv, mm_out, st.at[1])
    store_mw.start()
    store_mm.start()

    def partial(j, half):
        return lax.dot_general(
            xq[j, :, pl.ds(half * 128, 128)], uall[...], (((0,), (0,)), ((), ())), preferred_element_type=F32
        )

    def reduce(n, chain):
        sign, half, short = chain
        d = 0 if sign > 0 else 1
        return remote(
            rs_out.at[d, n - 1, short], rs_in.at[d, n - 1, short],
            rs_s.at[d, n - 1, short], rs_r.at[d, n - 1, short], along(sign),
        )

    def send_sum(n, chain):
        sign, half, short = chain
        d = 0 if sign > 0 else 1
        j = (z + 8 + sign * (5 - short - n)) % 8
        value = partial(j, half)
        if n > 1:
            reduce(n - 1, chain).wait_recv()
            value = value + rs_in[d, n - 2, short].astype(F32)
        rs_out[d, n - 1, short] = value.astype(BF16)
        reduce(n, chain).start()

    for k in (1, 2, 3):
        u_copy(k).wait_recv()

    @pl.loop(0, 8)
    def _(j):
        own_x(j).wait()
        for k in (1, 2, 3):
            x_copy(k, j).wait_recv()

    for chain in chains:
        send_sum(1, chain)

    for chain in chains[:2]:
        gather_in(4, chain).wait_recv()

    def b_copy(k, j):
        return remote(ub.at[j, k], uh.at[k, j], b_s.at[k - 1, j], b_r.at[k - 1, j], mate(k))

    @pl.loop(0, 8)
    def _(j):
        w = wq[j].reshape(F, K)
        u = lax.dot_general(uall[...], w, (((1,), (1,)), ((), ())), preferred_element_type=F32)
        ub[j] = u.astype(BF16).reshape(4, T, F)
        for k in (2, 3, 1):
            b_copy(k, j).start()
        gps[j] = jnp.sum(u * xq[j].astype(F32), axis=0, keepdims=True)

    def g_copy(s):
        return remote(gps.at[(z + s) % 8], gpr.at[s - 1], g_s.at[s - 1], g_r.at[s - 1], along(s))

    for s in range(1, 8):
        g_copy(s).start()

    for chain in chains:
        send_sum(2, chain)

    def k_copy(k):
        return remote(kvs.at[k], kvr.at[k - 1], k_s.at[k - 1], k_r.at[k - 1], mate(k))

    def kv_part(k):
        def add(j, acc):
            return acc + jnp.dot(
                xq[j, pl.ds(k * T, T), :], wq[j].reshape(F, K), preferred_element_type=F32
            )

        return lax.fori_loop(0, 8, add, jnp.zeros((T, K), F32))

    for k in (2, 3, 1):
        kvs[k] = kv_part(k).astype(BF16)
        k_copy(k).start()
    kvv[...] = kv_part(0)

    for chain in chains:
        send_sum(3, chain)

    @pl.loop(0, 8)
    def _(j):
        for k in (1, 2, 3):
            b_copy(k, j).wait_recv()

    def dots(j, acc):
        acc = acc + xv[:, column(0, j)].astype(F32) * ub[j, 0].astype(F32)
        for k in (1, 2, 3):
            acc = acc + xv[:, column(k, j)].astype(F32) * uh[k, j].astype(F32)
        return acc

    acc = lax.fori_loop(0, 8, dots, jnp.zeros((T, 256), F32))
    inverse = inv[...][:, :1]
    coefficient = jnp.sum(acc, axis=1, keepdims=True) * (1.0 / D) * inverse * inverse

    @pl.loop(0, 8)
    def _(j):
        for k in range(4):
            u = (ub[j, 0] if k == 0 else uh[k, j]).astype(F32)
            dxv[:, column(k, j)] = (u - xv[:, column(k, j)].astype(F32) * coefficient).astype(BF16)

    store_dx = pltpu.make_async_copy(dxv, dx_out, st.at[2])
    store_dx.start()

    for chain in chains[:2]:
        send_sum(4, chain)

    for k in (1, 2, 3):
        k_copy(k).wait_recv()
    total = kvv[...] + kvr[0].astype(F32) + kvr[1].astype(F32) + kvr[2].astype(F32)
    uv[...] = (total * inverse).astype(BF16)
    store_kv = pltpu.make_async_copy(uv, kv_out, st.at[3])
    store_kv.start()

    gain_sum = gps[z]
    for s in range(1, 8):
        g_copy(s).wait_recv()
    for s in range(1, 8):
        gain_sum = gain_sum + gpr[s - 1]
    gg_out[...] = gain_sum / gain_row

    for half in range(2):
        rows = pl.ds(half * 128, 128)
        value = partial(z, half)
        for chain in chains:
            if chain[1] == half:
                sign, _, short = chain
                d = 0 if sign > 0 else 1
                reduce(4 - short, chain).wait_recv()
                value = value + rs_in[d, 3 - short, short].astype(F32)
        g = gcol[rows, :]
        for t in range(8):
            dwv[rows, pl.ds(t * 128, 128)] = (value[:, t * 128 : t * 128 + 128] * g).astype(BF16)
    store_dw = pltpu.make_async_copy(dwv, dw_out, st.at[4])
    store_dw.start()

    for chain in chains:
        for n in range(1, 5 - chain[2]):
            gather(n, chain).wait_send()
            reduce(n, chain).wait_send()
    for k in (1, 2, 3):
        u_copy(k).wait_send()
        k_copy(k).wait_send()

    @pl.loop(0, 8)
    def _(j):
        for k in (1, 2, 3):
            x_copy(k, j).wait_send()
            b_copy(k, j).wait_send()

    for s in range(1, 8):
        g_copy(s).wait_send()
    for q in range(1, 4):
        d1_copy(q).wait_send()
        d3_copy(q).wait_send()
    d2_copy.wait_send()
    store_mw.wait()
    store_mm.wait()
    store_dx.wait()
    store_kv.wait()
    store_dw.wait()


def local(hidden, norm_gain, weight, upstream, global_weight, global_momentum, replica_delta):
    anywhere = pl.BlockSpec(memory_space=pl.ANY)
    in_vmem = pl.BlockSpec(memory_space=pltpu.VMEM)
    dma = pltpu.SemaphoreType.DMA
    kv, dx, dw, gg, mw, mm = pl.pallas_call(
        kernel,
        out_shape=(
            jax.ShapeDtypeStruct((T, K), BF16),
            jax.ShapeDtypeStruct((T, D), BF16),
            jax.ShapeDtypeStruct((F, K), BF16),
            jax.ShapeDtypeStruct((1, F), F32),
            jax.ShapeDtypeStruct((F, K), F32),
            jax.ShapeDtypeStruct((F, K), F32),
        ),
        in_specs=[anywhere, in_vmem] + [anywhere] * 5,
        out_specs=(anywhere, anywhere, anywhere, in_vmem, anywhere, anywhere),
        scratch_shapes=[
            pltpu.VMEM((T, D), BF16),
            pltpu.VMEM((8, 4 * T, F), BF16),
            pltpu.VMEM((F, K), BF16),
            pltpu.VMEM((8, 2, 128, K), BF16),
            pltpu.VMEM((T, K), BF16),
            pltpu.VMEM((4 * T, K), BF16),
            pltpu.VMEM((8, 4, T, F), BF16),
            pltpu.VMEM((4, 8, T, F), BF16),
            pltpu.VMEM((T, 128), F32),
            pltpu.VMEM((F, 128), F32),
            pltpu.VMEM((2, 4, 2, 128, K), BF16),
            pltpu.VMEM((2, 4, 2, 128, K), BF16),
            pltpu.VMEM((4, T, K), BF16),
            pltpu.VMEM((3, T, K), BF16),
            pltpu.VMEM((8, 1, F), F32),
            pltpu.VMEM((7, 1, F), F32),
            pltpu.VMEM((F, K), F32),
            pltpu.VMEM((F, K), BF16),
            pltpu.VMEM((3, R, K), BF16),
            pltpu.VMEM((R, K), BF16),
            pltpu.VMEM((R, K), BF16),
            pltpu.VMEM((F, K), BF16),
            pltpu.VMEM((F, K), F32),
            pltpu.VMEM((F, K), F32),
            pltpu.VMEM((T, D), BF16),
            pltpu.VMEM((F, K), BF16),
            pltpu.VMEM((T, K), F32),
            dma((6,)), dma((8,)), dma((5,)),
            dma((2, 4, 2)), dma((2, 4, 2)), dma((2, 4, 2)), dma((2, 4, 2)),
            dma((3, 8)), dma((3, 8)), dma((3,)), dma((3,)), dma((3, 8)), dma((3, 8)),
            dma((3,)), dma((3,)), dma((7,)), dma((7,)),
            dma((3,)), dma((3,)), dma, dma, dma((3,)), dma((3,)),
        ],
        compiler_params=pltpu.CompilerParams(
            collective_id=0, has_side_effects=True, vmem_limit_bytes=58 * 2**20
        ),
        cost_estimate=pl.CostEstimate(flops=6442450944, bytes_accessed=14 * 2**20, transcendentals=0),
        name="project",
    )(
        hidden[0], norm_gain, weight[0], upstream[0], replica_delta[0], global_weight, global_momentum
    )
    return kv[None], dx[None], dw[None], gg.astype(BF16), mw, mm


def solution(mesh):
    rows = P("replica", "fsdp", None)
    return jax.shard_map(
        local,
        mesh=mesh,
        in_specs=(rows, P("replica", "fsdp"), rows, rows, P("fsdp", None), P("fsdp", None), rows),
        out_specs=(rows, rows, rows, P("replica", "fsdp"), P("fsdp", None), P("fsdp", None)),
        check_vma=False,
    )
```

```python
import functools

import jax
import jax.numpy as jnp
from jax import lax
from jax.experimental import pallas as pl
from jax.experimental.pallas import tpu as pltpu
from jax.sharding import PartitionSpec as P

MESH = pl.DeviceIdType.MESH
F32 = jnp.float32
BF16 = jnp.bfloat16
T = 128
F = 256
K = 1024
D = 8192
R = 64


def device(h, z, c, low, x):
    return {"replica": low * 4 + x, "fsdp": h * 16 + z * 2 + c}


def kernel(
    x_hbm, gain_ref, w_hbm, u_hbm, delta_hbm, gw_hbm, gm_hbm,
    kv_out, dx_out, dw_out, gg_out, mw_out, mm_out,
    xv, xq, wv, wq, uv, uall, ub, uh, inv, gcol, rs_out, rs_in,
    kvs, kvr, gps, gpr, dv, dbf, d1, d2s, d2r, davg, gwv, gmv, kvv,
    ld, lq, ag_s, ag_r, rs_s, rs_r, x_s, x_r, u_s, u_r, b_s, b_r, k_s, k_r, g_s, g_r,
    d1_s, d1_r, d2_s, d2_r, d3_s, d3_r,
):
    fsdp, rep = lax.axis_index("fsdp"), lax.axis_index("replica")
    h, z, c = fsdp // 16, (fsdp % 16) // 2, fsdp % 2
    low, xx = rep // 4, rep % 4

    def mate(k):
        return device((h + k // 2) % 2, z, (c + k % 2) % 2, low, xx)

    def along(step):
        return device(h, (z + 8 + step) % 8, c, low, xx)

    def column(k, j):
        at = ((h + k // 2) % 2) * 4096 + j * 512 + ((c + k % 2) % 2) * 256
        return pl.ds(pl.multiple_of(at, 256), 256)

    def remote(src, dst, s, r, to):
        return pltpu.make_async_remote_copy(
            src_ref=src, dst_ref=dst, send_sem=s, recv_sem=r, device_id=to, device_id_type=MESH
        )

    load_w = pltpu.make_async_copy(w_hbm, wv, ld.at[0])
    load_u = pltpu.make_async_copy(u_hbm, uv, ld.at[1])
    load_x = pltpu.make_async_copy(x_hbm, xv, ld.at[2])
    load_d = pltpu.make_async_copy(delta_hbm, dv, ld.at[3])
    load_gw = pltpu.make_async_copy(gw_hbm, gwv, ld.at[4])
    load_gm = pltpu.make_async_copy(gm_hbm, gmv, ld.at[5])
    load_w.start()
    load_x.start()
    load_u.start()
    load_d.start()

    def own_x(j):
        return pltpu.make_async_copy(x_hbm.at[:, column(0, j)], xq.at[j, pl.ds(0, T)], lq.at[j])

    barrier = pltpu.get_barrier_semaphore()
    others = [along(s) for s in range(1, 8)] + [mate(k) for k in range(1, 4)]
    others += [device(h, z, c, low, (xx + q) % 4) for q in range(1, 4)]
    others += [device(h, z, c, 1 - low, xx)]
    for to in others:
        pl.semaphore_signal(barrier, inc=1, device_id=to, device_id_type=MESH)

    gain_row = gain_ref[...].astype(F32)
    gcol[...] = jnp.transpose(jnp.broadcast_to(gain_row, (128, F)))
    load_w.wait()
    for half in range(2):
        rows = pl.ds(half * 128, 128)
        g = gcol[rows, :]
        for t in range(8):
            cols = pl.ds(t * 128, 128)
            wq[z, half, :, cols] = (wv[rows, cols].astype(F32) * g).astype(BF16)
    pl.semaphore_wait(barrier, len(others))

    chains = [(1, 0, 0), (-1, 1, 0), (1, 1, 1), (-1, 0, 1)]

    def gather(n, chain):
        sign, half, short = chain
        d = 0 if sign > 0 else 1
        block = wq.at[(z + 8 - sign * (n - 1)) % 8, half]
        return remote(block, block, ag_s.at[d, n - 1, half], ag_r.at[d, n - 1, half], along(sign))

    def gather_in(n, chain):
        sign, half, short = chain
        d = 0 if sign > 0 else 1
        block = wq.at[(z + 8 - sign * n) % 8, half]
        return remote(block, block, ag_s.at[d, n - 1, half], ag_r.at[d, n - 1, half], along(sign))

    for chain in chains:
        gather(1, chain).start()

    def x_copy(k, j):
        return remote(
            x_hbm.at[:, column(k, j)], xq.at[j, pl.ds(k * T, T)], x_s.at[k - 1, j], x_r.at[k - 1, j], mate(k)
        )

    @pl.loop(0, 2)
    def _(j):
        for k in (2, 3):
            x_copy(k, j).start()

    def quarter(i):
        return pl.ds(pl.multiple_of(i * R, R), R)

    def d1_copy(q):
        to = (xx + q) % 4
        return remote(dbf.at[quarter(to)], d1.at[q - 1], d1_s.at[q - 1], d1_r.at[q - 1], device(h, z, c, low, to))

    load_d.wait()
    dbf[...] = dv[...].astype(BF16)
    for q in range(1, 4):
        d1_copy(q).start()

    load_x.wait()

    def squares(i, acc):
        v = xv[:, pl.ds(pl.multiple_of(i * 256, 256), 256)].astype(F32)
        return acc + v * v

    acc = lax.fori_loop(0, 32, squares, jnp.zeros((T, 256), F32))
    inverse = lax.rsqrt(jnp.sum(acc, axis=1, keepdims=True) * (1.0 / D) + 1e-05)
    inv[...] = jnp.broadcast_to(inverse, (T, 128))
    load_u.wait()
    uall[pl.ds(0, T), :] = (uv[...].astype(F32) * inverse).astype(BF16)

    def u_copy(k):
        near = 2 * T if k == 3 else 0
        to = mate(1) if k == 3 else mate(k)
        return remote(uall.at[pl.ds(near, T)], uall.at[pl.ds(k * T, T)], u_s.at[k - 1], u_r.at[k - 1], to)

    u_copy(2).start()
    u_copy(1).start()

    @pl.loop(2, 8)
    def _(j):
        for k in (2, 3):
            x_copy(k, j).start()

    @pl.loop(0, 8)
    def _(j):
        x_copy(1, j).start()
        own_x(j).start()

    load_gw.start()
    load_gm.start()

    def b_copy(k, j):
        return remote(ub.at[j, k], uh.at[k, j], b_s.at[k - 1, j], b_r.at[k - 1, j], mate(k))

    def upper(low_step, high_step):
        @pl.loop(low_step, high_step)
        def _(step):
            j = (z + 8 + step) % 8
            w = wq[j].reshape(F, K)
            u = lax.dot_general(uall[...], w, (((1,), (1,)), ((), ())), preferred_element_type=F32)
            ub[j] = u.astype(BF16).reshape(4, T, F)
            for k in (2, 3, 1):
                b_copy(k, j).start()

    def upper_pair(step):
        @pl.loop(0, 2)
        def _(i):
            j = (z + 8 + step - 2 * step * i) % 8
            w = wq[j].reshape(F, K)
            u = lax.dot_general(uall[...], w, (((1,), (1,)), ((), ())), preferred_element_type=F32)
            ub[j] = u.astype(BF16).reshape(4, T, F)
            for k in (2, 3, 1):
                b_copy(k, j).start()

    def hop(n):
        for chain in chains:
            gather_in(n, chain).wait_recv()
            if n < 3 or chain[2] == 0:
                gather(n + 1, chain).start()

    hop(1)

    d2_copy = remote(d2s, d2r, d2_s, d2_r, device(h, z, c, 1 - low, xx))
    for q in range(1, 4):
        d1_copy(q).wait_recv()
    d2s[...] = (
        dv[quarter(xx), :] + d1[0].astype(F32) + d1[1].astype(F32) + d1[2].astype(F32)
    ).astype(BF16)
    d2_copy.start()

    u_copy(2).wait_recv()
    u_copy(3).start()
    u_copy(1).wait_recv()
    u_copy(3).wait_recv()
    upper(-1, 2)

    hop(2)

    def d3_copy(q):
        block = davg.at[quarter(xx)]
        return remote(block, block, d3_s.at[q - 1], d3_r.at[q - 1], device(h, z, c, low, (xx + q) % 4))

    d2_copy.wait_recv()
    davg[quarter(xx), :] = ((d2s[...].astype(F32) + d2r[...].astype(F32)) * 0.125).astype(BF16)
    for q in range(1, 4):
        d3_copy(q).start()
    upper_pair(2)

    hop(3)
    upper_pair(3)

    def d3_in(q):
        block = davg.at[quarter((xx + 4 - q) % 4)]
        return remote(block, block, d3_s.at[q - 1], d3_r.at[q - 1], device(h, z, c, low, (xx + q) % 4))

    for q in range(1, 4):
        d3_in(q).wait_recv()
    load_gw.wait()
    load_gm.wait()

    @pl.loop(0, 8)
    def _(i):
        rows = pl.ds(pl.multiple_of(i * 32, 32), 32)
        average = davg[rows, :].astype(F32)
        fresh = 0.9 * gmv[rows, :] + average
        mm_out[rows, :] = fresh
        mw_out[rows, :] = gwv[rows, :] - 0.7 * (average + 0.9 * fresh)

    def partial(j, half):
        return lax.dot_general(
            xq[j, :, pl.ds(half * 128, 128)], uall[...], (((0,), (0,)), ((), ())), preferred_element_type=F32
        )

    def reduce(n, chain):
        sign, half, short = chain
        d = 0 if sign > 0 else 1
        return remote(
            rs_out.at[d, n - 1, short], rs_in.at[d, n - 1, short],
            rs_s.at[d, n - 1, short], rs_r.at[d, n - 1, short], along(sign),
        )

    def send_sum(n, chain):
        sign, half, short = chain
        d = 0 if sign > 0 else 1
        j = (z + 8 + sign * (5 - short - n)) % 8
        value = partial(j, half)
        if n > 1:
            reduce(n - 1, chain).wait_recv()
            value = value + rs_in[d, n - 2, short].astype(F32)
        rs_out[d, n - 1, short] = value.astype(BF16)
        reduce(n, chain).start()

    @pl.loop(0, 8)
    def _(j):
        own_x(j).wait()
        for k in (1, 2, 3):
            x_copy(k, j).wait_recv()

    for chain in chains:
        send_sum(1, chain)

    for chain in chains[:2]:
        gather_in(4, chain).wait_recv()

    upper(4, 5)

    @pl.loop(0, 8)
    def _(j):
        u = ub[j].reshape(4 * T, F).astype(F32)
        gps[j] = jnp.sum(u * xq[j].astype(F32), axis=0, keepdims=True)

    def g_copy(s):
        return remote(gps.at[(z + s) % 8], gpr.at[s - 1], g_s.at[s - 1], g_r.at[s - 1], along(s))

    for s in range(1, 8):
        g_copy(s).start()

    for chain in chains:
        send_sum(2, chain)

    def k_copy(k):
        to = mate(1) if k == 3 else mate(k)
        return remote(kvs.at[k], kvr.at[k - 1], k_s.at[k - 1], k_r.at[k - 1], to)

    def kv_part(k):
        def add(j, acc):
            return acc + jnp.dot(
                xq[j, pl.ds(k * T, T), :], wq[j].reshape(F, K), preferred_element_type=F32
            )

        return lax.fori_loop(0, 8, add, jnp.zeros((T, K), F32))

    kvs[3] = kv_part(3).astype(BF16)
    k_copy(3).start()
    kvs[1] = kv_part(1).astype(BF16)
    k_copy(1).start()
    value = kv_part(2)
    k_copy(3).wait_recv()
    kvs[2] = (value + kvr[2].astype(F32)).astype(BF16)
    k_copy(2).start()
    kvv[...] = kv_part(0)

    for chain in chains:
        send_sum(3, chain)

    @pl.loop(0, 8)
    def _(j):
        for k in (1, 2, 3):
            b_copy(k, j).wait_recv()

    def dots(j, acc):
        acc = acc + xv[:, column(0, j)].astype(F32) * ub[j, 0].astype(F32)
        for k in (1, 2, 3):
            acc = acc + xv[:, column(k, j)].astype(F32) * uh[k, j].astype(F32)
        return acc

    acc = lax.fori_loop(0, 8, dots, jnp.zeros((T, 256), F32))
    inverse = inv[...][:, :1]
    coefficient = jnp.sum(acc, axis=1, keepdims=True) * (1.0 / D) * inverse * inverse

    @pl.loop(0, 8)
    def _(j):
        for k in range(4):
            u = (ub[j, 0] if k == 0 else uh[k, j]).astype(F32)
            dx_out[:, column(k, j)] = (u - xv[:, column(k, j)].astype(F32) * coefficient).astype(BF16)

    for chain in chains[:2]:
        send_sum(4, chain)

    for k in (1, 2):
        k_copy(k).wait_recv()
    total = kvv[...] + kvr[0].astype(F32) + kvr[1].astype(F32)
    kv_out[...] = (total * inverse).astype(BF16)

    gain_sum = gps[z]
    for s in range(1, 8):
        g_copy(s).wait_recv()
    for s in range(1, 8):
        gain_sum = gain_sum + gpr[s - 1]
    gg_out[...] = (gain_sum / gain_row).astype(BF16)

    for half in range(2):
        rows = pl.ds(half * 128, 128)
        value = partial(z, half)
        for chain in chains:
            if chain[1] == half:
                sign, _, short = chain
                d = 0 if sign > 0 else 1
                reduce(4 - short, chain).wait_recv()
                value = value + rs_in[d, 3 - short, short].astype(F32)
        g = gcol[rows, :]
        for t in range(8):
            dw_out[rows, pl.ds(t * 128, 128)] = (value[:, t * 128 : t * 128 + 128] * g).astype(BF16)

    for chain in chains:
        for n in range(1, 5 - chain[2]):
            gather(n, chain).wait_send()
            reduce(n, chain).wait_send()
    for k in (1, 2, 3):
        u_copy(k).wait_send()
        k_copy(k).wait_send()

    @pl.loop(0, 8)
    def _(j):
        for k in (1, 2, 3):
            x_copy(k, j).wait_send()
            b_copy(k, j).wait_send()

    for s in range(1, 8):
        g_copy(s).wait_send()
    for q in range(1, 4):
        d1_copy(q).wait_send()
        d3_copy(q).wait_send()
    d2_copy.wait_send()


def finish(*refs):
    copies = [pltpu.make_async_copy(refs[i], refs[6 + i], refs[12].at[i]) for i in range(6)]
    for copy in copies:
        copy.start()
    for copy in copies:
        copy.wait()


def local(hidden, norm_gain, weight, upstream, global_weight, global_momentum, replica_delta):
    anywhere = pl.BlockSpec(memory_space=pl.ANY)
    in_vmem = pl.BlockSpec(memory_space=pltpu.VMEM)
    in_hbm = pl.BlockSpec(memory_space=pltpu.HBM)
    dma = pltpu.SemaphoreType.DMA
    results = pl.pallas_call(
        kernel,
        out_shape=(
            pltpu.VMEM((T, K), BF16),
            pltpu.VMEM((T, D), BF16),
            pltpu.VMEM((F, K), BF16),
            pltpu.VMEM((1, F), BF16),
            pltpu.VMEM((F, K), F32),
            pltpu.VMEM((F, K), F32),
        ),
        in_specs=[in_hbm, in_vmem] + [in_hbm] * 5,
        out_specs=(in_vmem,) * 6,
        scratch_shapes=[
            pltpu.VMEM((T, D), BF16),
            pltpu.VMEM((8, 4 * T, F), BF16),
            pltpu.VMEM((F, K), BF16),
            pltpu.VMEM((8, 2, 128, K), BF16),
            pltpu.VMEM((T, K), BF16),
            pltpu.VMEM((4 * T, K), BF16),
            pltpu.VMEM((8, 4, T, F), BF16),
            pltpu.VMEM((4, 8, T, F), BF16),
            pltpu.VMEM((T, 128), F32),
            pltpu.VMEM((F, 128), F32),
            pltpu.VMEM((2, 4, 2, 128, K), BF16),
            pltpu.VMEM((2, 4, 2, 128, K), BF16),
            pltpu.VMEM((4, T, K), BF16),
            pltpu.VMEM((3, T, K), BF16),
            pltpu.VMEM((8, 1, F), F32),
            pltpu.VMEM((7, 1, F), F32),
            pltpu.VMEM((F, K), F32),
            pltpu.VMEM((F, K), BF16),
            pltpu.VMEM((3, R, K), BF16),
            pltpu.VMEM((R, K), BF16),
            pltpu.VMEM((R, K), BF16),
            pltpu.VMEM((F, K), BF16),
            pltpu.VMEM((F, K), F32),
            pltpu.VMEM((F, K), F32),
            pltpu.VMEM((T, K), F32),
            dma((6,)), dma((8,)),
            dma((2, 4, 2)), dma((2, 4, 2)), dma((2, 4, 2)), dma((2, 4, 2)),
            dma((3, 8)), dma((3, 8)), dma((3,)), dma((3,)), dma((3, 8)), dma((3, 8)),
            dma((3,)), dma((3,)), dma((7,)), dma((7,)),
            dma((3,)), dma((3,)), dma, dma, dma((3,)), dma((3,)),
        ],
        compiler_params=pltpu.CompilerParams(
            collective_id=0, has_side_effects=True, vmem_limit_bytes=59 * 2**20
        ),
        cost_estimate=pl.CostEstimate(flops=6442450944, bytes_accessed=14 * 2**20, transcendentals=0),
        name="project",
    )(
        hidden[0], norm_gain, weight[0], upstream[0], replica_delta[0], global_weight, global_momentum
    )
    kv, dx, dw, gg, mw, mm = pl.pallas_call(
        finish,
        out_shape=tuple(jax.ShapeDtypeStruct(r.shape, r.dtype) for r in results),
        in_specs=[in_vmem] * 6,
        out_specs=(anywhere,) * 6,
        scratch_shapes=[dma((6,))],
        compiler_params=pltpu.CompilerParams(vmem_limit_bytes=8 * 2**20),
        name="finish",
    )(*results)
    return kv[None], dx[None], dw[None], gg, mw, mm


def solution(mesh):
    rows = P("replica", "fsdp", None)
    return jax.shard_map(
        local,
        mesh=mesh,
        in_specs=(rows, P("replica", "fsdp"), rows, rows, P("fsdp", None), P("fsdp", None), rows),
        out_specs=(rows, rows, rows, P("replica", "fsdp"), P("fsdp", None), P("fsdp", None)),
        check_vma=False,
    )
```

```python
import functools

import jax
import jax.numpy as jnp
from jax import lax
from jax.experimental import pallas as pl
from jax.experimental.pallas import tpu as pltpu
from jax.sharding import PartitionSpec as P

MESH = pl.DeviceIdType.MESH
F32 = jnp.float32
BF16 = jnp.bfloat16
T = 128
F = 256
K = 1024
D = 8192
R = 64


def device(h, z, c, low, x):
    return {"replica": low * 4 + x, "fsdp": h * 16 + z * 2 + c}


def kernel(
    x_hbm, gain_ref, w_hbm, u_hbm, delta_hbm, gw_hbm, gm_hbm,
    kv_out, dx_out, dw_out, gg_out, mw_out, mm_out,
    xv, xq, wq, uv, uall, ub, uh, inv, gcol, rs_out, rs_in,
    kvs, kvr, gps, gpr, gall, sums, dv, dbf, d1, d2s, d2r, davg, gwv, gmv, kvv,
    ld, lq, ag_s, ag_r, rs_s, rs_r, x_s, x_r, u_s, u_r, b_s, b_r, k_s, k_r, g_s, g_r, n_s, n_r,
    d1_s, d1_r, d2_s, d2_r, d3_s, d3_r,
):
    fsdp, rep = lax.axis_index("fsdp"), lax.axis_index("replica")
    h, z, c = fsdp // 16, (fsdp % 16) // 2, fsdp % 2
    low, xx = rep // 4, rep % 4

    def mate(k):
        return device((h + k // 2) % 2, z, (c + k % 2) % 2, low, xx)

    def along(step):
        return device(h, (z + 8 + step) % 8, c, low, xx)

    def column(k, j):
        at = ((h + k // 2) % 2) * 4096 + j * 512 + ((c + k % 2) % 2) * 256
        return pl.ds(pl.multiple_of(at, 256), 256)

    def remote(src, dst, s, r, to):
        return pltpu.make_async_remote_copy(
            src_ref=src, dst_ref=dst, send_sem=s, recv_sem=r, device_id=to, device_id_type=MESH
        )

    def w_half(half):
        return w_hbm.at[pl.ds(half * 128, 128)]

    load_w = [pltpu.make_async_copy(w_half(i), wq.at[z, i], ld.at[6 * i]) for i in range(2)]
    load_u = pltpu.make_async_copy(u_hbm, uv, ld.at[1])
    load_x = pltpu.make_async_copy(x_hbm, xv, ld.at[2])
    load_d = pltpu.make_async_copy(delta_hbm, dv, ld.at[3])
    load_gw = pltpu.make_async_copy(gw_hbm, gwv, ld.at[4])
    load_gm = pltpu.make_async_copy(gm_hbm, gmv, ld.at[5])

    def own_x(j):
        return pltpu.make_async_copy(x_hbm.at[:, column(0, j)], xq.at[j, pl.ds(0, T)], lq.at[j])

    barrier = pltpu.get_barrier_semaphore()
    others = [along(s) for s in range(1, 8)] + [mate(k) for k in range(1, 4)]
    others += [device(h, z, c, low, (xx + q) % 4) for q in range(1, 4)]
    others += [device(h, z, c, 1 - low, xx)]
    for to in others:
        pl.semaphore_signal(barrier, inc=1, device_id=to, device_id_type=MESH)

    load_x.start()
    load_u.start()
    load_d.start()
    for copy in load_w:
        copy.start()
    gain_row = gain_ref[...].astype(F32)
    gall[z] = gain_row
    pl.semaphore_wait(barrier, len(others))

    chains = [(1, 0, 0), (-1, 1, 0), (1, 1, 1), (-1, 0, 1)]

    def gather(n, chain):
        sign, half, short = chain
        d = 0 if sign > 0 else 1
        block = wq.at[(z + 8 - sign * (n - 1)) % 8, half]
        return remote(w_half(half) if n == 1 else block, block, ag_s.at[d, n - 1, half], ag_r.at[d, n - 1, half], along(sign))

    def gather_in(n, chain):
        sign, half, short = chain
        d = 0 if sign > 0 else 1
        block = wq.at[(z + 8 - sign * n) % 8, half]
        return remote(block, block, ag_s.at[d, n - 1, half], ag_r.at[d, n - 1, half], along(sign))

    for chain in chains:
        gather(1, chain).start()

    def n_copy(s, owner):
        block = gall.at[(z + 8 + owner) % 8]
        return remote(block, block, n_s.at[s - 1], n_r.at[s - 1], along(s))

    for s in range(1, 8):
        n_copy(s, 0).start()

    def gain_of(*steps):
        for step in steps:
            n_copy((-step) % 8, step).wait_recv()

    def x_copy(k, j):
        return remote(
            x_hbm.at[:, column(k, j)], xq.at[j, pl.ds(k * T, T)], x_s.at[k - 1, j], x_r.at[k - 1, j], mate(k)
        )

    @pl.loop(0, 2)
    def _(j):
        for k in (2, 3):
            x_copy(k, j).start()

    def quarter(i):
        return pl.ds(pl.multiple_of(i * R, R), R)

    def d1_copy(q):
        to = (xx + q) % 4
        return remote(dbf.at[quarter(to)], d1.at[q - 1], d1_s.at[q - 1], d1_r.at[q - 1], device(h, z, c, low, to))

    load_d.wait()
    dbf[...] = dv[...].astype(BF16)
    for q in range(1, 4):
        d1_copy(q).start()

    load_x.wait()

    def squares(i, acc):
        v = xv[:, pl.ds(pl.multiple_of(i * 256, 256), 256)].astype(F32)
        return acc + v * v

    acc = lax.fori_loop(0, 32, squares, jnp.zeros((T, 256), F32))
    inverse = lax.rsqrt(jnp.sum(acc, axis=1, keepdims=True) * (1.0 / D) + 1e-05)
    inv[...] = jnp.broadcast_to(inverse, (T, 128))
    load_u.wait()
    uall[pl.ds(0, T), :] = (uv[...].astype(F32) * inverse).astype(BF16)

    def u_copy(k):
        near = 2 * T if k == 3 else 0
        to = mate(1) if k == 3 else mate(k)
        return remote(uall.at[pl.ds(near, T)], uall.at[pl.ds(k * T, T)], u_s.at[k - 1], u_r.at[k - 1], to)

    u_copy(2).start()
    u_copy(1).start()

    @pl.loop(2, 8)
    def _(j):
        for k in (2, 3):
            x_copy(k, j).start()

    @pl.loop(0, 8)
    def _(j):
        x_copy(1, j).start()
        own_x(j).start()

    load_gw.start()
    load_gm.start()

    def b_copy(k, j):
        return remote(ub.at[j, k], uh.at[k, j], b_s.at[k - 1, j], b_r.at[k - 1, j], mate(k))

    def upper(low_step, high_step):
        @pl.loop(low_step, high_step)
        def _(step):
            j = (z + 8 + step) % 8
            w = wq[j].reshape(F, K)
            u = lax.dot_general(uall[...], w, (((1,), (1,)), ((), ())), preferred_element_type=F32)
            u = u * gall[j]
            ub[j] = u.astype(BF16).reshape(4, T, F)
            for k in (2, 3, 1):
                b_copy(k, j).start()

    def upper_pair(step):
        @pl.loop(0, 2)
        def _(i):
            j = (z + 8 + step - 2 * step * i) % 8
            w = wq[j].reshape(F, K)
            u = lax.dot_general(uall[...], w, (((1,), (1,)), ((), ())), preferred_element_type=F32)
            u = u * gall[j]
            ub[j] = u.astype(BF16).reshape(4, T, F)
            for k in (2, 3, 1):
                b_copy(k, j).start()

    def hop(n):
        for chain in chains:
            gather_in(n, chain).wait_recv()
            if n < 3 or chain[2] == 0:
                gather(n + 1, chain).start()

    hop(1)

    d2_copy = remote(d2s, d2r, d2_s, d2_r, device(h, z, c, 1 - low, xx))
    for q in range(1, 4):
        d1_copy(q).wait_recv()
    d2s[...] = (
        dv[quarter(xx), :] + d1[0].astype(F32) + d1[1].astype(F32) + d1[2].astype(F32)
    ).astype(BF16)
    d2_copy.start()

    u_copy(2).wait_recv()
    u_copy(3).start()
    u_copy(1).wait_recv()
    u_copy(3).wait_recv()
    for copy in load_w:
        copy.wait()
    gain_of(-1, 1)
    upper(-1, 2)

    hop(2)

    def d3_copy(q):
        block = davg.at[quarter(xx)]
        return remote(block, block, d3_s.at[q - 1], d3_r.at[q - 1], device(h, z, c, low, (xx + q) % 4))

    d2_copy.wait_recv()
    davg[quarter(xx), :] = ((d2s[...].astype(F32) + d2r[...].astype(F32)) * 0.125).astype(BF16)
    for q in range(1, 4):
        d3_copy(q).start()
    gain_of(-2, 2)
    upper_pair(2)

    hop(3)
    gain_of(-3, 3)
    upper_pair(3)

    def d3_in(q):
        block = davg.at[quarter((xx + 4 - q) % 4)]
        return remote(block, block, d3_s.at[q - 1], d3_r.at[q - 1], device(h, z, c, low, (xx + q) % 4))

    for q in range(1, 4):
        d3_in(q).wait_recv()
    load_gw.wait()
    load_gm.wait()

    @pl.loop(0, 8)
    def _(i):
        rows = pl.ds(pl.multiple_of(i * 32, 32), 32)
        average = davg[rows, :].astype(F32)
        fresh = 0.9 * gmv[rows, :] + average
        mm_out[rows, :] = fresh
        mw_out[rows, :] = gwv[rows, :] - 0.7 * (average + 0.9 * fresh)

    def partial(j, half):
        return lax.dot_general(
            xq[j, :, pl.ds(half * 128, 128)], uall[...], (((0,), (0,)), ((), ())), preferred_element_type=F32
        )

    def reduce(n, chain):
        sign, half, short = chain
        d = 0 if sign > 0 else 1
        return remote(
            rs_out.at[d, n - 1, short], rs_in.at[d, n - 1, short],
            rs_s.at[d, n - 1, short], rs_r.at[d, n - 1, short], along(sign),
        )

    def prepare(n):
        for i, (sign, half, short) in enumerate(chains):
            if n < 5 - short:
                sums[i] = partial((z + 8 + sign * (5 - short - n)) % 8, half)

    def send_sum(n, chain):
        sign, half, short = chain
        d = 0 if sign > 0 else 1
        value = sums[chains.index(chain)]
        if n > 1:
            reduce(n - 1, chain).wait_recv()
            value = value + rs_in[d, n - 2, short].astype(F32)
        rs_out[d, n - 1, short] = value.astype(BF16)
        reduce(n, chain).start()

    @pl.loop(0, 8)
    def _(j):
        own_x(j).wait()
        for k in (1, 2, 3):
            x_copy(k, j).wait_recv()

    prepare(1)
    for chain in chains:
        send_sum(1, chain)

    for chain in chains[:2]:
        gather_in(4, chain).wait_recv()

    gain_of(4)
    upper(4, 5)

    @pl.loop(0, 8)
    def _(j):
        u = ub[j].reshape(4 * T, F).astype(F32)
        gps[j] = jnp.sum(u * xq[j].astype(F32), axis=0, keepdims=True)

    def g_copy(s):
        return remote(gps.at[(z + s) % 8], gpr.at[s - 1], g_s.at[s - 1], g_r.at[s - 1], along(s))

    for s in range(1, 8):
        g_copy(s).start()

    prepare(2)
    for chain in chains:
        send_sum(2, chain)

    def k_copy(k):
        to = mate(1) if k == 3 else mate(k)
        return remote(kvs.at[k], kvr.at[k - 1], k_s.at[k - 1], k_r.at[k - 1], to)

    def kv_part(k):
        def add(j, acc):
            x = (xq[j, pl.ds(k * T, T), :].astype(F32) * gall[j]).astype(BF16)
            return acc + jnp.dot(x, wq[j].reshape(F, K), preferred_element_type=F32)

        return lax.fori_loop(0, 8, add, jnp.zeros((T, K), F32))

    kvs[3] = kv_part(3).astype(BF16)
    k_copy(3).start()
    kvs[1] = kv_part(1).astype(BF16)
    k_copy(1).start()
    value = kv_part(2)
    k_copy(3).wait_recv()
    kvs[2] = (value + kvr[2].astype(F32)).astype(BF16)
    k_copy(2).start()
    kvv[...] = kv_part(0)

    prepare(3)
    for chain in chains:
        send_sum(3, chain)

    @pl.loop(0, 8)
    def _(j):
        for k in (1, 2, 3):
            b_copy(k, j).wait_recv()

    def dots(j, acc):
        acc = acc + xv[:, column(0, j)].astype(F32) * ub[j, 0].astype(F32)
        for k in (1, 2, 3):
            acc = acc + xv[:, column(k, j)].astype(F32) * uh[k, j].astype(F32)
        return acc

    acc = lax.fori_loop(0, 8, dots, jnp.zeros((T, 256), F32))
    inverse = inv[...][:, :1]
    coefficient = jnp.sum(acc, axis=1, keepdims=True) * (1.0 / D) * inverse * inverse

    @pl.loop(0, 8)
    def _(j):
        for k in range(4):
            u = (ub[j, 0] if k == 0 else uh[k, j]).astype(F32)
            dx_out[:, column(k, j)] = (u - xv[:, column(k, j)].astype(F32) * coefficient).astype(BF16)

    prepare(4)
    for chain in chains[:2]:
        send_sum(4, chain)

    for half in range(2):
        sums[half] = partial(z, half)
    gcol[...] = jnp.transpose(jnp.broadcast_to(gain_row, (128, F)))

    for k in (1, 2):
        k_copy(k).wait_recv()
    total = kvv[...] + kvr[0].astype(F32) + kvr[1].astype(F32)
    kv_out[...] = (total * inverse).astype(BF16)

    gain_sum = gps[z]
    for s in range(1, 8):
        g_copy(s).wait_recv()
    for s in range(1, 8):
        gain_sum = gain_sum + gpr[s - 1]
    gg_out[...] = (gain_sum / gain_row).astype(BF16)

    for half in range(2):
        rows = pl.ds(half * 128, 128)
        value = sums[half]
        for chain in chains:
            if chain[1] == half:
                sign, _, short = chain
                d = 0 if sign > 0 else 1
                reduce(4 - short, chain).wait_recv()
                value = value + rs_in[d, 3 - short, short].astype(F32)
        g = gcol[rows, :]
        for t in range(8):
            dw_out[rows, pl.ds(t * 128, 128)] = (value[:, t * 128 : t * 128 + 128] * g).astype(BF16)

    for chain in chains:
        for n in range(1, 5 - chain[2]):
            gather(n, chain).wait_send()
            reduce(n, chain).wait_send()
    for k in (1, 2, 3):
        u_copy(k).wait_send()
        k_copy(k).wait_send()

    @pl.loop(0, 8)
    def _(j):
        for k in (1, 2, 3):
            x_copy(k, j).wait_send()
            b_copy(k, j).wait_send()

    for s in range(1, 8):
        g_copy(s).wait_send()
        n_copy(s, 0).wait_send()
    for q in range(1, 4):
        d1_copy(q).wait_send()
        d3_copy(q).wait_send()
    d2_copy.wait_send()


def finish(*refs):
    copies = []
    for i, parts in enumerate((1, 4, 1, 1, 2, 2)):
        rows = refs[i].shape[0] // parts
        for part in range(parts):
            at = pl.ds(part * rows, rows)
            copies.append(pltpu.make_async_copy(refs[i].at[at], refs[6 + i].at[at], refs[12].at[len(copies)]))
    for copy in copies:
        copy.start()
    for copy in copies:
        copy.wait()


def local(hidden, norm_gain, weight, upstream, global_weight, global_momentum, replica_delta):
    anywhere = pl.BlockSpec(memory_space=pl.ANY)
    in_vmem = pl.BlockSpec(memory_space=pltpu.VMEM)
    in_hbm = pl.BlockSpec(memory_space=pltpu.HBM)
    dma = pltpu.SemaphoreType.DMA
    results = pl.pallas_call(
        kernel,
        out_shape=(
            pltpu.VMEM((T, K), BF16),
            pltpu.VMEM((T, D), BF16),
            pltpu.VMEM((F, K), BF16),
            pltpu.VMEM((1, F), BF16),
            pltpu.VMEM((F, K), F32),
            pltpu.VMEM((F, K), F32),
        ),
        in_specs=[in_hbm, in_vmem] + [in_hbm] * 5,
        out_specs=(in_vmem,) * 6,
        scratch_shapes=[
            pltpu.VMEM((T, D), BF16),
            pltpu.VMEM((8, 4 * T, F), BF16),
            pltpu.VMEM((8, 2, 128, K), BF16),
            pltpu.VMEM((T, K), BF16),
            pltpu.VMEM((4 * T, K), BF16),
            pltpu.VMEM((8, 4, T, F), BF16),
            pltpu.VMEM((4, 8, T, F), BF16),
            pltpu.VMEM((T, 128), F32),
            pltpu.VMEM((F, 128), F32),
            pltpu.VMEM((2, 4, 2, 128, K), BF16),
            pltpu.VMEM((2, 4, 2, 128, K), BF16),
            pltpu.VMEM((4, T, K), BF16),
            pltpu.VMEM((3, T, K), BF16),
            pltpu.VMEM((8, 1, F), F32),
            pltpu.VMEM((7, 1, F), F32),
            pltpu.VMEM((8, 1, F), F32),
            pltpu.VMEM((4, 128, K), F32),
            pltpu.VMEM((F, K), F32),
            pltpu.VMEM((F, K), BF16),
            pltpu.VMEM((3, R, K), BF16),
            pltpu.VMEM((R, K), BF16),
            pltpu.VMEM((R, K), BF16),
            pltpu.VMEM((F, K), BF16),
            pltpu.VMEM((F, K), F32),
            pltpu.VMEM((F, K), F32),
            pltpu.VMEM((T, K), F32),
            dma((7,)), dma((8,)),
            dma((2, 4, 2)), dma((2, 4, 2)), dma((2, 4, 2)), dma((2, 4, 2)),
            dma((3, 8)), dma((3, 8)), dma((3,)), dma((3,)), dma((3, 8)), dma((3, 8)),
            dma((3,)), dma((3,)), dma((7,)), dma((7,)), dma((7,)), dma((7,)),
            dma((3,)), dma((3,)), dma, dma, dma((3,)), dma((3,)),
        ],
        compiler_params=pltpu.CompilerParams(
            collective_id=0, has_side_effects=True, vmem_limit_bytes=59 * 2**20
        ),
        cost_estimate=pl.CostEstimate(flops=6442450944, bytes_accessed=14 * 2**20, transcendentals=0),
        name="project",
    )(
        hidden[0], norm_gain, weight[0], upstream[0], replica_delta[0], global_weight, global_momentum
    )
    kv, dx, dw, gg, mw, mm = pl.pallas_call(
        finish,
        out_shape=tuple(jax.ShapeDtypeStruct(r.shape, r.dtype) for r in results),
        in_specs=[in_vmem] * 6,
        out_specs=(anywhere,) * 6,
        scratch_shapes=[dma((11,))],
        compiler_params=pltpu.CompilerParams(vmem_limit_bytes=8 * 2**20),
        name="finish",
    )(*results)
    return kv[None], dx[None], dw[None], gg, mw, mm


def solution(mesh):
    rows = P("replica", "fsdp", None)
    return jax.shard_map(
        local,
        mesh=mesh,
        in_specs=(rows, P("replica", "fsdp"), rows, rows, P("fsdp", None), P("fsdp", None), rows),
        out_specs=(rows, rows, rows, P("replica", "fsdp"), P("fsdp", None), P("fsdp", None)),
        check_vma=False,
    )
```

```python
import functools

import jax
import jax.numpy as jnp
from jax import lax
from jax.experimental import pallas as pl
from jax.experimental.pallas import tpu as pltpu
from jax.sharding import PartitionSpec as P

MESH = pl.DeviceIdType.MESH
F32 = jnp.float32
BF16 = jnp.bfloat16
T = 128
F = 256
K = 1024
D = 8192
R = 64


def device(h, z, c, low, x):
    return {"replica": low * 4 + x, "fsdp": h * 16 + z * 2 + c}


def kernel(
    x_hbm, gain_ref, w_hbm, u_hbm, delta_hbm, gw_hbm, gm_hbm,
    kv_out, dx_out, dw_out, gg_out, mw_out, mm_out,
    xv, xq, wq, uv, uall, ub, uh, inv, gcol, rs_out, rs_in,
    kvs, kvr, gps, gpr, gall, sums, dv, dbf, d1, d2s, d2r, davg, gwv, gmv, kvv,
    ld, lq, ag_s, ag_r, rs_s, rs_r, x_s, x_r, u_s, u_r, b_s, b_r, k_s, k_r, g_s, g_r, n_s, n_r,
    d1_s, d1_r, d2_s, d2_r, d3_s, d3_r, ready,
):
    fsdp, rep = lax.axis_index("fsdp"), lax.axis_index("replica")
    h, z, c = fsdp // 16, (fsdp % 16) // 2, fsdp % 2
    low, xx = rep // 4, rep % 4

    def mate(k):
        return device((h + k // 2) % 2, z, (c + k % 2) % 2, low, xx)

    def along(step):
        return device(h, (z + 8 + step) % 8, c, low, xx)

    def column(k, j):
        at = ((h + k // 2) % 2) * 4096 + j * 512 + ((c + k % 2) % 2) * 256
        return pl.ds(pl.multiple_of(at, 256), 256)

    def remote(src, dst, s, r, to):
        return pltpu.make_async_remote_copy(
            src_ref=src, dst_ref=dst, send_sem=s, recv_sem=r, device_id=to, device_id_type=MESH
        )

    def w_half(half):
        return w_hbm.at[pl.ds(half * 128, 128)]

    load_w = [pltpu.make_async_copy(w_half(i), wq.at[z, i], ld.at[6 * i]) for i in range(2)]
    load_u = pltpu.make_async_copy(u_hbm, uv, ld.at[1])
    load_x = pltpu.make_async_copy(x_hbm, xv, ld.at[2])
    load_d = pltpu.make_async_copy(delta_hbm, dv, ld.at[3])
    load_gw = pltpu.make_async_copy(gw_hbm, gwv, ld.at[4])
    load_gm = pltpu.make_async_copy(gm_hbm, gmv, ld.at[5])

    def own_x(j):
        return pltpu.make_async_copy(x_hbm.at[:, column(0, j)], xq.at[j, pl.ds(0, T)], lq.at[j])

    barrier = pltpu.get_barrier_semaphore()
    hubs = [device(1 - h, z, 1, low, xx), device(h, z, 1, 1 - low, xx)]
    hubs += [device(h, z, 1, low, (xx + q) % 4) for q in range(1, 4)]
    for to in [along(1), along(-1)] + hubs:
        pl.semaphore_signal(barrier, inc=1, device_id=to, device_id_type=MESH)

    @pl.when(c == 0)
    def _():
        pl.semaphore_signal(barrier, inc=1, device_id=mate(1), device_id_type=MESH)

    load_x.start()
    load_u.start()
    load_d.start()
    for copy in load_w:
        copy.start()
    gain_row = gain_ref[...].astype(F32)
    gall[z] = gain_row
    @pl.when(c == 0)
    def _():
        pl.semaphore_wait(barrier, 2)

    @pl.when(c == 1)
    def _():
        pl.semaphore_wait(barrier, 3 + 2 * len(hubs))
        pl.semaphore_signal(ready, inc=1, device_id=mate(1), device_id_type=MESH)

    chains = [(1, 0, 0), (-1, 1, 0), (1, 1, 1), (-1, 0, 1)]

    def gather(n, chain):
        sign, half, short = chain
        d = 0 if sign > 0 else 1
        block = wq.at[(z + 8 - sign * (n - 1)) % 8, half]
        return remote(w_half(half) if n == 1 else block, block, ag_s.at[d, n - 1, half], ag_r.at[d, n - 1, half], along(sign))

    def gather_in(n, chain):
        sign, half, short = chain
        d = 0 if sign > 0 else 1
        block = wq.at[(z + 8 - sign * n) % 8, half]
        return remote(block, block, ag_s.at[d, n - 1, half], ag_r.at[d, n - 1, half], along(sign))

    for chain in chains:
        gather(1, chain).start()

    def n_copy(n, sign, arriving=0):
        d = 0 if sign > 0 else 1
        block = gall.at[(z + 8 - sign * (n - 1 + arriving)) % 8]
        return remote(block, block, n_s.at[d, n - 1], n_r.at[d, n - 1], along(sign))

    for sign in (1, -1):
        n_copy(1, sign).start()

    @pl.when(c == 0)
    def _():
        pl.semaphore_wait(ready, 1)

    def x_copy(k, j):
        return remote(
            x_hbm.at[:, column(k, j)], xq.at[j, pl.ds(k * T, T)], x_s.at[k - 1, j], x_r.at[k - 1, j], mate(k)
        )

    @pl.loop(0, 2)
    def _(j):
        for k in (2, 3):
            x_copy(k, j).start()

    def quarter(i):
        return pl.ds(pl.multiple_of(i * R, R), R)

    def d1_copy(q):
        to = (xx + q) % 4
        return remote(dbf.at[quarter(to)], d1.at[q - 1], d1_s.at[q - 1], d1_r.at[q - 1], device(h, z, c, low, to))

    load_d.wait()
    dbf[...] = dv[...].astype(BF16)
    for q in range(1, 4):
        d1_copy(q).start()

    load_x.wait()

    def squares(i, acc):
        v = xv[:, pl.ds(pl.multiple_of(i * 256, 256), 256)].astype(F32)
        return acc + v * v

    acc = lax.fori_loop(0, 32, squares, jnp.zeros((T, 256), F32))
    inverse = lax.rsqrt(jnp.sum(acc, axis=1, keepdims=True) * (1.0 / D) + 1e-05)
    inv[...] = jnp.broadcast_to(inverse, (T, 128))
    load_u.wait()
    uall[pl.ds(0, T), :] = (uv[...].astype(F32) * inverse).astype(BF16)

    def u_copy(k):
        near = 2 * T if k == 3 else 0
        to = mate(1) if k == 3 else mate(k)
        return remote(uall.at[pl.ds(near, T)], uall.at[pl.ds(k * T, T)], u_s.at[k - 1], u_r.at[k - 1], to)

    u_copy(2).start()
    u_copy(1).start()

    @pl.loop(2, 8)
    def _(j):
        for k in (2, 3):
            x_copy(k, j).start()

    @pl.loop(0, 8)
    def _(j):
        x_copy(1, j).start()
        own_x(j).start()

    load_gw.start()
    load_gm.start()

    def b_copy(k, j):
        return remote(ub.at[j, k], uh.at[k, j], b_s.at[k - 1, j], b_r.at[k - 1, j], mate(k))

    def upper(low_step, high_step):
        @pl.loop(low_step, high_step)
        def _(step):
            j = (z + 8 + step) % 8
            w = wq[j].reshape(F, K)
            u = lax.dot_general(uall[...], w, (((1,), (1,)), ((), ())), preferred_element_type=F32)
            u = u * gall[j]
            ub[j] = u.astype(BF16).reshape(4, T, F)
            for k in (2, 3, 1):
                b_copy(k, j).start()

    def upper_pair(step):
        @pl.loop(0, 2)
        def _(i):
            j = (z + 8 + step - 2 * step * i) % 8
            w = wq[j].reshape(F, K)
            u = lax.dot_general(uall[...], w, (((1,), (1,)), ((), ())), preferred_element_type=F32)
            u = u * gall[j]
            ub[j] = u.astype(BF16).reshape(4, T, F)
            for k in (2, 3, 1):
                b_copy(k, j).start()

    def hop(n):
        for chain in chains:
            gather_in(n, chain).wait_recv()
            if n < 3 or chain[2] == 0:
                gather(n + 1, chain).start()
        for sign in (1, -1):
            n_copy(n, sign, 1).wait_recv()
            if n < 3 or sign > 0:
                n_copy(n + 1, sign).start()

    hop(1)

    d2_copy = remote(d2s, d2r, d2_s, d2_r, device(h, z, c, 1 - low, xx))
    for q in range(1, 4):
        d1_copy(q).wait_recv()
    d2s[...] = (
        dv[quarter(xx), :] + d1[0].astype(F32) + d1[1].astype(F32) + d1[2].astype(F32)
    ).astype(BF16)
    d2_copy.start()

    u_copy(2).wait_recv()
    u_copy(3).start()
    u_copy(1).wait_recv()
    u_copy(3).wait_recv()
    for copy in load_w:
        copy.wait()
    upper(-1, 2)

    hop(2)

    def d3_copy(q):
        block = davg.at[quarter(xx)]
        return remote(block, block, d3_s.at[q - 1], d3_r.at[q - 1], device(h, z, c, low, (xx + q) % 4))

    d2_copy.wait_recv()
    davg[quarter(xx), :] = ((d2s[...].astype(F32) + d2r[...].astype(F32)) * 0.125).astype(BF16)
    for q in range(1, 4):
        d3_copy(q).start()
    upper_pair(2)

    def partial(j, half):
        return lax.dot_general(
            xq[j, :, pl.ds(half * 128, 128)], uall[...], (((0,), (0,)), ((), ())), preferred_element_type=F32
        )

    def reduce(n, chain):
        sign, half, short = chain
        d = 0 if sign > 0 else 1
        return remote(
            rs_out.at[d, n - 1, short], rs_in.at[d, n - 1, short],
            rs_s.at[d, n - 1, short], rs_r.at[d, n - 1, short], along(sign),
        )

    def prepare(n):
        for i, (sign, half, short) in enumerate(chains):
            if n < 5 - short:
                sums[i] = partial((z + 8 + sign * (5 - short - n)) % 8, half)

    def send_sum(n, chain):
        sign, half, short = chain
        d = 0 if sign > 0 else 1
        value = sums[chains.index(chain)]
        if n > 1:
            reduce(n - 1, chain).wait_recv()
            value = value + rs_in[d, n - 2, short].astype(F32)
        rs_out[d, n - 1, short] = value.astype(BF16)
        reduce(n, chain).start()

    def first_sums():
        @pl.loop(0, 8)
        def _(j):
            own_x(j).wait()
            for k in (1, 2, 3):
                x_copy(k, j).wait_recv()

        prepare(1)
        for chain in chains:
            send_sum(1, chain)

    pl.when(c == 0)(first_sums)

    hop(3)
    upper_pair(3)

    def d3_in(q):
        block = davg.at[quarter((xx + 4 - q) % 4)]
        return remote(block, block, d3_s.at[q - 1], d3_r.at[q - 1], device(h, z, c, low, (xx + q) % 4))

    for q in range(1, 4):
        d3_in(q).wait_recv()
    load_gw.wait()
    load_gm.wait()

    @pl.loop(0, 8)
    def _(i):
        rows = pl.ds(pl.multiple_of(i * 32, 32), 32)
        average = davg[rows, :].astype(F32)
        fresh = 0.9 * gmv[rows, :] + average
        mm_out[rows, :] = fresh
        mw_out[rows, :] = gwv[rows, :] - 0.7 * (average + 0.9 * fresh)

    pl.when(c == 1)(first_sums)

    for chain in chains[:2]:
        gather_in(4, chain).wait_recv()

    n_copy(4, 1, 1).wait_recv()
    upper(4, 5)

    @pl.loop(0, 8)
    def _(j):
        u = ub[j].reshape(4 * T, F).astype(F32)
        gps[j] = jnp.sum(u * xq[j].astype(F32), axis=0, keepdims=True)

    def g_copy(s):
        return remote(gps.at[(z + s) % 8], gpr.at[s - 1], g_s.at[s - 1], g_r.at[s - 1], along(s))

    for s in range(1, 8):
        g_copy(s).start()

    prepare(2)
    for chain in chains:
        send_sum(2, chain)

    def k_copy(k):
        to = mate(1) if k == 3 else mate(k)
        return remote(kvs.at[k], kvr.at[k - 1], k_s.at[k - 1], k_r.at[k - 1], to)

    def kv_part(k):
        def add(j, acc):
            x = (xq[j, pl.ds(k * T, T), :].astype(F32) * gall[j]).astype(BF16)
            return acc + jnp.dot(x, wq[j].reshape(F, K), preferred_element_type=F32)

        return lax.fori_loop(0, 8, add, jnp.zeros((T, K), F32))

    kvs[3] = kv_part(3).astype(BF16)
    k_copy(3).start()
    kvs[1] = kv_part(1).astype(BF16)
    k_copy(1).start()
    value = kv_part(2)
    k_copy(3).wait_recv()
    kvs[2] = (value + kvr[2].astype(F32)).astype(BF16)
    k_copy(2).start()
    kvv[...] = kv_part(0)

    prepare(3)
    for chain in chains:
        send_sum(3, chain)

    @pl.loop(0, 8)
    def _(j):
        for k in (1, 2, 3):
            b_copy(k, j).wait_recv()

    def dots(j, acc):
        acc = acc + xv[:, column(0, j)].astype(F32) * ub[j, 0].astype(F32)
        for k in (1, 2, 3):
            acc = acc + xv[:, column(k, j)].astype(F32) * uh[k, j].astype(F32)
        return acc

    acc = lax.fori_loop(0, 8, dots, jnp.zeros((T, 256), F32))
    inverse = inv[...][:, :1]
    coefficient = jnp.sum(acc, axis=1, keepdims=True) * (1.0 / D) * inverse * inverse

    @pl.loop(0, 8)
    def _(j):
        for k in range(4):
            u = (ub[j, 0] if k == 0 else uh[k, j]).astype(F32)
            dx_out[:, column(k, j)] = (u - xv[:, column(k, j)].astype(F32) * coefficient).astype(BF16)

    prepare(4)
    for chain in chains[:2]:
        send_sum(4, chain)

    for half in range(2):
        sums[half] = partial(z, half)
    gcol[...] = jnp.transpose(jnp.broadcast_to(gain_row, (128, F)))

    for k in (1, 2):
        k_copy(k).wait_recv()
    total = kvv[...] + kvr[0].astype(F32) + kvr[1].astype(F32)
    kv_out[...] = (total * inverse).astype(BF16)

    gain_sum = gps[z]
    for s in range(1, 8):
        g_copy(s).wait_recv()
    for s in range(1, 8):
        gain_sum = gain_sum + gpr[s - 1]
    gg_out[...] = (gain_sum / gain_row).astype(BF16)

    for half in range(2):
        rows = pl.ds(half * 128, 128)
        value = sums[half]
        for chain in chains:
            if chain[1] == half:
                sign, _, short = chain
                d = 0 if sign > 0 else 1
                reduce(4 - short, chain).wait_recv()
                value = value + rs_in[d, 3 - short, short].astype(F32)
        g = gcol[rows, :]
        for t in range(8):
            dw_out[rows, pl.ds(t * 128, 128)] = (value[:, t * 128 : t * 128 + 128] * g).astype(BF16)

    for chain in chains:
        for n in range(1, 5 - chain[2]):
            gather(n, chain).wait_send()
            reduce(n, chain).wait_send()
    for k in (1, 2, 3):
        u_copy(k).wait_send()
        k_copy(k).wait_send()

    @pl.loop(0, 8)
    def _(j):
        for k in (1, 2, 3):
            x_copy(k, j).wait_send()
            b_copy(k, j).wait_send()

    for s in range(1, 8):
        g_copy(s).wait_send()
        n_copy((s + 1) // 2, 1 if s % 2 else -1).wait_send()
    for q in range(1, 4):
        d1_copy(q).wait_send()
        d3_copy(q).wait_send()
    d2_copy.wait_send()


def finish(*refs):
    copies = []
    for i, parts in enumerate((1, 4, 1, 1, 2, 2)):
        rows = refs[i].shape[0] // parts
        for part in range(parts):
            at = pl.ds(part * rows, rows)
            copies.append(pltpu.make_async_copy(refs[i].at[at], refs[6 + i].at[at], refs[12].at[len(copies)]))
    for copy in copies:
        copy.start()
    for copy in copies:
        copy.wait()


def local(hidden, norm_gain, weight, upstream, global_weight, global_momentum, replica_delta):
    anywhere = pl.BlockSpec(memory_space=pl.ANY)
    in_vmem = pl.BlockSpec(memory_space=pltpu.VMEM)
    in_hbm = pl.BlockSpec(memory_space=pltpu.HBM)
    dma = pltpu.SemaphoreType.DMA
    results = pl.pallas_call(
        kernel,
        out_shape=(
            pltpu.VMEM((T, K), BF16),
            pltpu.VMEM((T, D), BF16),
            pltpu.VMEM((F, K), BF16),
            pltpu.VMEM((1, F), BF16),
            pltpu.VMEM((F, K), F32),
            pltpu.VMEM((F, K), F32),
        ),
        in_specs=[in_hbm, in_vmem] + [in_hbm] * 5,
        out_specs=(in_vmem,) * 6,
        scratch_shapes=[
            pltpu.VMEM((T, D), BF16),
            pltpu.VMEM((8, 4 * T, F), BF16),
            pltpu.VMEM((8, 2, 128, K), BF16),
            pltpu.VMEM((T, K), BF16),
            pltpu.VMEM((4 * T, K), BF16),
            pltpu.VMEM((8, 4, T, F), BF16),
            pltpu.VMEM((4, 8, T, F), BF16),
            pltpu.VMEM((T, 128), F32),
            pltpu.VMEM((F, 128), F32),
            pltpu.VMEM((2, 4, 2, 128, K), BF16),
            pltpu.VMEM((2, 4, 2, 128, K), BF16),
            pltpu.VMEM((4, T, K), BF16),
            pltpu.VMEM((3, T, K), BF16),
            pltpu.VMEM((8, 1, F), F32),
            pltpu.VMEM((7, 1, F), F32),
            pltpu.VMEM((8, 1, F), F32),
            pltpu.VMEM((4, 128, K), F32),
            pltpu.VMEM((F, K), F32),
            pltpu.VMEM((F, K), BF16),
            pltpu.VMEM((3, R, K), BF16),
            pltpu.VMEM((R, K), BF16),
            pltpu.VMEM((R, K), BF16),
            pltpu.VMEM((F, K), BF16),
            pltpu.VMEM((F, K), F32),
            pltpu.VMEM((F, K), F32),
            pltpu.VMEM((T, K), F32),
            dma((7,)), dma((8,)),
            dma((2, 4, 2)), dma((2, 4, 2)), dma((2, 4, 2)), dma((2, 4, 2)),
            dma((3, 8)), dma((3, 8)), dma((3,)), dma((3,)), dma((3, 8)), dma((3, 8)),
            dma((3,)), dma((3,)), dma((7,)), dma((7,)), dma((2, 4)), dma((2, 4)),
            dma((3,)), dma((3,)), dma, dma, dma((3,)), dma((3,)),
            pltpu.SemaphoreType.REGULAR,
        ],
        compiler_params=pltpu.CompilerParams(
            collective_id=0, has_side_effects=True, vmem_limit_bytes=59 * 2**20
        ),
        cost_estimate=pl.CostEstimate(flops=6442450944, bytes_accessed=14 * 2**20, transcendentals=0),
        name="project",
    )(
        hidden[0], norm_gain, weight[0], upstream[0], replica_delta[0], global_weight, global_momentum
    )
    kv, dx, dw, gg, mw, mm = pl.pallas_call(
        finish,
        out_shape=tuple(jax.ShapeDtypeStruct(r.shape, r.dtype) for r in results),
        in_specs=[in_vmem] * 6,
        out_specs=(anywhere,) * 6,
        scratch_shapes=[dma((11,))],
        compiler_params=pltpu.CompilerParams(vmem_limit_bytes=8 * 2**20),
        name="finish",
    )(*results)
    return kv[None], dx[None], dw[None], gg, mw, mm


def solution(mesh):
    rows = P("replica", "fsdp", None)
    return jax.shard_map(
        local,
        mesh=mesh,
        in_specs=(rows, P("replica", "fsdp"), rows, rows, P("fsdp", None), P("fsdp", None), rows),
        out_specs=(rows, rows, rows, P("replica", "fsdp"), P("fsdp", None), P("fsdp", None)),
        check_vma=False,
    )
```

```python
import functools

import jax
import jax.numpy as jnp
from jax import lax
from jax.experimental import pallas as pl
from jax.experimental.pallas import tpu as pltpu
from jax.sharding import PartitionSpec as P

MESH = pl.DeviceIdType.MESH
F32 = jnp.float32
BF16 = jnp.bfloat16
T = 128
F = 256
K = 1024
D = 8192
R = 64


def device(h, z, c, low, x):
    return {"replica": low * 4 + x, "fsdp": h * 16 + z * 2 + c}


def kernel(
    x_hbm, gain_ref, w_hbm, u_hbm, delta_hbm, gw_hbm, gm_hbm,
    kv_out, dx_out, dw_out, gg_out, mw_out, mm_out,
    xv, xq, wq, uv, uall, ub, uh, inv, gcol, rs_out, rs_in,
    kvs, kvr, gps, gpr, gall, sums, dv, dbf, d1, d2s, d2r, davg, gwv, gmv, kvv,
    ld, lq, ag_s, ag_r, rs_s, rs_r, x_s, x_r, u_s, u_r, b_s, b_r, k_s, k_r, g_s, g_r, n_s, n_r,
    d1_s, d1_r, d2_s, d2_r, d3_s, d3_r, ready,
):
    fsdp, rep = lax.axis_index("fsdp"), lax.axis_index("replica")
    h, z, c = fsdp // 16, (fsdp % 16) // 2, fsdp % 2
    low, xx = rep // 4, rep % 4

    def mate(k):
        return device((h + k // 2) % 2, z, (c + k % 2) % 2, low, xx)

    def along(step):
        return device(h, (z + 8 + step) % 8, c, low, xx)

    def column(k, j):
        at = ((h + k // 2) % 2) * 4096 + j * 512 + ((c + k % 2) % 2) * 256
        return pl.ds(pl.multiple_of(at, 256), 256)

    def remote(src, dst, s, r, to):
        return pltpu.make_async_remote_copy(
            src_ref=src, dst_ref=dst, send_sem=s, recv_sem=r, device_id=to, device_id_type=MESH
        )

    def w_half(half):
        return w_hbm.at[pl.ds(half * 128, 128)]

    load_w = [pltpu.make_async_copy(w_half(i), wq.at[z, i], ld.at[6 * i]) for i in range(2)]
    load_u = pltpu.make_async_copy(u_hbm, uv, ld.at[1])
    load_x = pltpu.make_async_copy(x_hbm, xv, ld.at[2])
    load_d = pltpu.make_async_copy(delta_hbm, dv, ld.at[3])
    load_gw = pltpu.make_async_copy(gw_hbm, gwv, ld.at[4])
    load_gm = pltpu.make_async_copy(gm_hbm, gmv, ld.at[5])

    def own_x(j):
        return pltpu.make_async_copy(x_hbm.at[:, column(0, j)], xq.at[j, pl.ds(0, T)], lq.at[j])

    barrier = pltpu.get_barrier_semaphore()
    hubs = [device(1 - h, z, 1, low, xx), device(h, z, 1, 1 - low, xx)]
    hubs += [device(h, z, 1, low, (xx + q) % 4) for q in range(1, 4)]
    for to in [along(1), along(-1)] + hubs:
        pl.semaphore_signal(barrier, inc=1, device_id=to, device_id_type=MESH)

    @pl.when(c == 0)
    def _():
        pl.semaphore_signal(barrier, inc=1, device_id=mate(1), device_id_type=MESH)

    load_x.start()
    load_u.start()
    load_d.start()
    for copy in load_w:
        copy.start()
    gain_row = gain_ref[...].astype(F32)
    gall[z] = gain_row
    @pl.when(c == 0)
    def _():
        pl.semaphore_wait(barrier, 2)

    @pl.when(c == 1)
    def _():
        pl.semaphore_wait(barrier, 3 + 2 * len(hubs))
        pl.semaphore_signal(ready, inc=1, device_id=mate(1), device_id_type=MESH)

    chains = [(1, 0, 0), (-1, 1, 0), (1, 1, 1), (-1, 0, 1)]

    def gather(n, chain):
        sign, half, short = chain
        d = 0 if sign > 0 else 1
        block = wq.at[(z + 8 - sign * (n - 1)) % 8, half]
        return remote(w_half(half) if n == 1 else block, block, ag_s.at[d, n - 1, half], ag_r.at[d, n - 1, half], along(sign))

    def gather_in(n, chain):
        sign, half, short = chain
        d = 0 if sign > 0 else 1
        block = wq.at[(z + 8 - sign * n) % 8, half]
        return remote(block, block, ag_s.at[d, n - 1, half], ag_r.at[d, n - 1, half], along(sign))

    for chain in chains:
        gather(1, chain).start()

    def n_copy(n, sign, arriving=0):
        d = 0 if sign > 0 else 1
        block = gall.at[(z + 8 - sign * (n - 1 + arriving)) % 8]
        return remote(block, block, n_s.at[d, n - 1], n_r.at[d, n - 1], along(sign))

    for sign in (1, -1):
        n_copy(1, sign).start()

    @pl.when(c == 0)
    def _():
        pl.semaphore_wait(ready, 1)

    def x_copy(k, j):
        return remote(
            x_hbm.at[:, column(k, j)], xq.at[j, pl.ds(k * T, T)], x_s.at[k - 1, j], x_r.at[k - 1, j], mate(k)
        )

    @pl.loop(0, 2)
    def _(j):
        for k in (2, 3):
            x_copy(k, j).start()

    def quarter(i):
        return pl.ds(pl.multiple_of(i * R, R), R)

    def d1_copy(q):
        to = (xx + q) % 4
        return remote(dbf.at[quarter(to)], d1.at[q - 1], d1_s.at[q - 1], d1_r.at[q - 1], device(h, z, c, low, to))

    load_d.wait()
    dbf[...] = dv[...].astype(BF16)
    for q in range(1, 4):
        d1_copy(q).start()

    load_x.wait()

    def squares(i, acc):
        v = xv[:, pl.ds(pl.multiple_of(i * 256, 256), 256)].astype(F32)
        return acc + v * v

    acc = lax.fori_loop(0, 32, squares, jnp.zeros((T, 256), F32))
    inverse = lax.rsqrt(jnp.sum(acc, axis=1, keepdims=True) * (1.0 / D) + 1e-05)
    inv[...] = jnp.broadcast_to(inverse, (T, 128))
    load_u.wait()
    uall[pl.ds(0, T), :] = (uv[...].astype(F32) * inverse).astype(BF16)

    def u_copy(k):
        near = 2 * T if k == 3 else 0
        to = mate(1) if k == 3 else mate(k)
        return remote(uall.at[pl.ds(near, T)], uall.at[pl.ds(k * T, T)], u_s.at[k - 1], u_r.at[k - 1], to)

    u_copy(2).start()
    u_copy(1).start()

    @pl.loop(2, 8)
    def _(j):
        for k in (2, 3):
            x_copy(k, j).start()

    @pl.loop(0, 8)
    def _(j):
        x_copy(1, j).start()
        own_x(j).start()

    load_gw.start()
    load_gm.start()

    def b_copy(k, j):
        return remote(ub.at[j, k], uh.at[k, j], b_s.at[k - 1, j], b_r.at[k - 1, j], mate(k))

    def upper(low_step, high_step):
        @pl.loop(low_step, high_step)
        def _(step):
            j = (z + 8 + step) % 8
            w = wq[j].reshape(F, K)
            u = lax.dot_general(uall[...], w, (((1,), (1,)), ((), ())), preferred_element_type=F32)
            u = u * gall[j]
            ub[j] = u.astype(BF16).reshape(4, T, F)
            for k in (2, 3, 1):
                b_copy(k, j).start()

    def upper_pair(step):
        @pl.loop(0, 2)
        def _(i):
            j = (z + 8 + step - 2 * step * i) % 8
            w = wq[j].reshape(F, K)
            u = lax.dot_general(uall[...], w, (((1,), (1,)), ((), ())), preferred_element_type=F32)
            u = u * gall[j]
            ub[j] = u.astype(BF16).reshape(4, T, F)
            for k in (2, 3, 1):
                b_copy(k, j).start()

    def hop(n):
        for chain in chains:
            gather_in(n, chain).wait_recv()
            if n < 3 or chain[2] == 0:
                gather(n + 1, chain).start()
        for sign in (1, -1):
            n_copy(n, sign, 1).wait_recv()
            if n < 3 or sign > 0:
                n_copy(n + 1, sign).start()

    hop(1)

    d2_copy = remote(d2s, d2r, d2_s, d2_r, device(h, z, c, 1 - low, xx))
    for q in range(1, 4):
        d1_copy(q).wait_recv()
    d2s[...] = (
        dv[quarter(xx), :] + d1[0].astype(F32) + d1[1].astype(F32) + d1[2].astype(F32)
    ).astype(BF16)
    d2_copy.start()

    u_copy(2).wait_recv()
    u_copy(3).start()
    u_copy(1).wait_recv()
    u_copy(3).wait_recv()
    for copy in load_w:
        copy.wait()
    upper(-1, 2)

    hop(2)

    def d3_copy(q):
        block = davg.at[quarter(xx)]
        return remote(block, block, d3_s.at[q - 1], d3_r.at[q - 1], device(h, z, c, low, (xx + q) % 4))

    d2_copy.wait_recv()
    davg[quarter(xx), :] = ((d2s[...].astype(F32) + d2r[...].astype(F32)) * 0.125).astype(BF16)
    for q in range(1, 4):
        d3_copy(q).start()
    upper_pair(2)

    def partial(j, half):
        return lax.dot_general(
            xq[j, :, pl.ds(half * 128, 128)], uall[...], (((0,), (0,)), ((), ())), preferred_element_type=F32
        )

    def reduce(n, chain):
        sign, half, short = chain
        d = 0 if sign > 0 else 1
        return remote(
            rs_out.at[d, n - 1, short], rs_in.at[d, n - 1, short],
            rs_s.at[d, n - 1, short], rs_r.at[d, n - 1, short], along(sign),
        )

    def prepare(n):
        for i, (sign, half, short) in enumerate(chains):
            if n < 5 - short:
                sums[i] = partial((z + 8 + sign * (5 - short - n)) % 8, half)

    def send_sum(n, chain):
        sign, half, short = chain
        d = 0 if sign > 0 else 1
        value = sums[chains.index(chain)]
        if n > 1:
            reduce(n - 1, chain).wait_recv()
            value = value + rs_in[d, n - 2, short].astype(F32)
        rs_out[d, n - 1, short] = value.astype(BF16)
        reduce(n, chain).start()

    def first_sums():
        @pl.loop(0, 8)
        def _(j):
            own_x(j).wait()
            for k in (1, 2, 3):
                x_copy(k, j).wait_recv()

        prepare(1)
        for chain in chains:
            send_sum(1, chain)

    pl.when(c == 0)(first_sums)

    hop(3)
    upper_pair(3)

    def d3_in(q):
        block = davg.at[quarter((xx + 4 - q) % 4)]
        return remote(block, block, d3_s.at[q - 1], d3_r.at[q - 1], device(h, z, c, low, (xx + q) % 4))

    for q in range(1, 4):
        d3_in(q).wait_recv()
    load_gw.wait()
    load_gm.wait()

    @pl.loop(0, 8)
    def _(i):
        rows = pl.ds(pl.multiple_of(i * 32, 32), 32)
        average = davg[rows, :].astype(F32)
        fresh = 0.9 * gmv[rows, :] + average
        mm_out[rows, :] = fresh
        mw_out[rows, :] = gwv[rows, :] - 0.7 * (average + 0.9 * fresh)

    pl.when(c == 1)(first_sums)

    for chain in chains[:2]:
        gather_in(4, chain).wait_recv()

    n_copy(4, 1, 1).wait_recv()
    upper(4, 5)

    @pl.loop(0, 8)
    def _(j):
        u = ub[j].reshape(4 * T, F).astype(F32)
        gps[j] = jnp.sum(u * xq[j].astype(F32), axis=0, keepdims=True)

    def g_copy(s):
        return remote(gps.at[(z + s) % 8], gpr.at[s - 1], g_s.at[s - 1], g_r.at[s - 1], along(s))

    for s in range(1, 8):
        g_copy(s).start()

    prepare(2)
    for chain in chains:
        send_sum(2, chain)

    def k_copy(k):
        to = mate(1) if k == 3 else mate(k)
        return remote(kvs.at[k], kvr.at[k - 1], k_s.at[k - 1], k_r.at[k - 1], to)

    def kv_part(k):
        def add(j, acc):
            x = (xq[j, pl.ds(k * T, T), :].astype(F32) * gall[j]).astype(BF16)
            return acc + jnp.dot(x, wq[j].reshape(F, K), preferred_element_type=F32)

        return lax.fori_loop(0, 8, add, jnp.zeros((T, K), F32))

    kvs[3] = kv_part(3).astype(BF16)
    k_copy(3).start()
    kvs[1] = kv_part(1).astype(BF16)
    k_copy(1).start()
    value = kv_part(2)
    k_copy(3).wait_recv()
    kvs[2] = (value + kvr[2].astype(F32)).astype(BF16)
    k_copy(2).start()
    kvv[...] = kv_part(0)

    prepare(3)
    for chain in chains:
        send_sum(3, chain)

    @pl.loop(0, 8)
    def _(j):
        for k in (1, 2, 3):
            b_copy(k, j).wait_recv()

    def dots(j, acc):
        acc = acc + xv[:, column(0, j)].astype(F32) * ub[j, 0].astype(F32)
        for k in (1, 2, 3):
            acc = acc + xv[:, column(k, j)].astype(F32) * uh[k, j].astype(F32)
        return acc

    acc = lax.fori_loop(0, 8, dots, jnp.zeros((T, 256), F32))
    inverse = inv[...][:, :1]
    coefficient = jnp.sum(acc, axis=1, keepdims=True) * (1.0 / D) * inverse * inverse

    @pl.loop(0, 8)
    def _(j):
        for k in range(4):
            u = (ub[j, 0] if k == 0 else uh[k, j]).astype(F32)
            dx_out[:, column(k, j)] = (u - xv[:, column(k, j)].astype(F32) * coefficient).astype(BF16)

    prepare(4)
    for chain in chains[:2]:
        send_sum(4, chain)

    for half in range(2):
        sums[half] = partial(z, half)
    gcol[...] = jnp.transpose(jnp.broadcast_to(gain_row, (128, F)))

    for k in (1, 2):
        k_copy(k).wait_recv()
    total = kvv[...] + kvr[0].astype(F32) + kvr[1].astype(F32)
    kv_out[...] = (total * inverse).astype(BF16)

    gain_sum = gps[z]
    for s in range(1, 8):
        g_copy(s).wait_recv()
    for s in range(1, 8):
        gain_sum = gain_sum + gpr[s - 1]
    gg_out[...] = (gain_sum / gain_row).astype(BF16)

    for chain in chains:
        for n in range(1, 5 - chain[2]):
            gather(n, chain).wait_send()
            if n < 4 - chain[2]:
                reduce(n, chain).wait_send()
    for k in (1, 2, 3):
        u_copy(k).wait_send()
        k_copy(k).wait_send()

    @pl.loop(0, 8)
    def _(j):
        for k in (1, 2, 3):
            x_copy(k, j).wait_send()
            b_copy(k, j).wait_send()

    for s in range(1, 8):
        g_copy(s).wait_send()
        n_copy((s + 1) // 2, 1 if s % 2 else -1).wait_send()
    for q in range(1, 4):
        d1_copy(q).wait_send()
        d3_copy(q).wait_send()
    d2_copy.wait_send()

    for half in range(2):
        rows = pl.ds(half * 128, 128)
        value = sums[half]
        for chain in chains:
            if chain[1] == half:
                sign, _, short = chain
                d = 0 if sign > 0 else 1
                reduce(4 - short, chain).wait_recv()
                value = value + rs_in[d, 3 - short, short].astype(F32)
        g = gcol[rows, :]
        for t in range(8):
            dw_out[rows, pl.ds(t * 128, 128)] = (value[:, t * 128 : t * 128 + 128] * g).astype(BF16)
    for chain in chains:
        reduce(4 - chain[2], chain).wait_send()


def finish(*refs):
    copies = []
    for i, parts in enumerate((1, 4, 1, 1, 2, 2)):
        rows = refs[i].shape[0] // parts
        for part in range(parts):
            at = pl.ds(part * rows, rows)
            copies.append(pltpu.make_async_copy(refs[i].at[at], refs[6 + i].at[at], refs[12].at[len(copies)]))
    for copy in copies:
        copy.start()
    for copy in copies:
        copy.wait()


def local(hidden, norm_gain, weight, upstream, global_weight, global_momentum, replica_delta):
    anywhere = pl.BlockSpec(memory_space=pl.ANY)
    in_vmem = pl.BlockSpec(memory_space=pltpu.VMEM)
    in_hbm = pl.BlockSpec(memory_space=pltpu.HBM)
    dma = pltpu.SemaphoreType.DMA
    results = pl.pallas_call(
        kernel,
        out_shape=(
            pltpu.VMEM((T, K), BF16),
            pltpu.VMEM((T, D), BF16),
            pltpu.VMEM((F, K), BF16),
            pltpu.VMEM((1, F), BF16),
            pltpu.VMEM((F, K), F32),
            pltpu.VMEM((F, K), F32),
        ),
        in_specs=[in_hbm, in_vmem] + [in_hbm] * 5,
        out_specs=(in_vmem,) * 6,
        scratch_shapes=[
            pltpu.VMEM((T, D), BF16),
            pltpu.VMEM((8, 4 * T, F), BF16),
            pltpu.VMEM((8, 2, 128, K), BF16),
            pltpu.VMEM((T, K), BF16),
            pltpu.VMEM((4 * T, K), BF16),
            pltpu.VMEM((8, 4, T, F), BF16),
            pltpu.VMEM((4, 8, T, F), BF16),
            pltpu.VMEM((T, 128), F32),
            pltpu.VMEM((F, 128), F32),
            pltpu.VMEM((2, 4, 2, 128, K), BF16),
            pltpu.VMEM((2, 4, 2, 128, K), BF16),
            pltpu.VMEM((4, T, K), BF16),
            pltpu.VMEM((3, T, K), BF16),
            pltpu.VMEM((8, 1, F), F32),
            pltpu.VMEM((7, 1, F), F32),
            pltpu.VMEM((8, 1, F), F32),
            pltpu.VMEM((4, 128, K), F32),
            pltpu.VMEM((F, K), F32),
            pltpu.VMEM((F, K), BF16),
            pltpu.VMEM((3, R, K), BF16),
            pltpu.VMEM((R, K), BF16),
            pltpu.VMEM((R, K), BF16),
            pltpu.VMEM((F, K), BF16),
            pltpu.VMEM((F, K), F32),
            pltpu.VMEM((F, K), F32),
            pltpu.VMEM((T, K), F32),
            dma((7,)), dma((8,)),
            dma((2, 4, 2)), dma((2, 4, 2)), dma((2, 4, 2)), dma((2, 4, 2)),
            dma((3, 8)), dma((3, 8)), dma((3,)), dma((3,)), dma((3, 8)), dma((3, 8)),
            dma((3,)), dma((3,)), dma((7,)), dma((7,)), dma((2, 4)), dma((2, 4)),
            dma((3,)), dma((3,)), dma, dma, dma((3,)), dma((3,)),
            pltpu.SemaphoreType.REGULAR,
        ],
        compiler_params=pltpu.CompilerParams(
            collective_id=0, has_side_effects=True, vmem_limit_bytes=59 * 2**20
        ),
        cost_estimate=pl.CostEstimate(flops=6442450944, bytes_accessed=14 * 2**20, transcendentals=0),
        name="project",
    )(
        hidden[0], norm_gain, weight[0], upstream[0], replica_delta[0], global_weight, global_momentum
    )
    kv, dx, dw, gg, mw, mm = pl.pallas_call(
        finish,
        out_shape=tuple(jax.ShapeDtypeStruct(r.shape, r.dtype) for r in results),
        in_specs=[in_vmem] * 6,
        out_specs=(anywhere,) * 6,
        scratch_shapes=[dma((11,))],
        compiler_params=pltpu.CompilerParams(vmem_limit_bytes=8 * 2**20),
        name="finish",
    )(*results)
    return kv[None], dx[None], dw[None], gg, mw, mm


def solution(mesh):
    rows = P("replica", "fsdp", None)
    return jax.shard_map(
        local,
        mesh=mesh,
        in_specs=(rows, P("replica", "fsdp"), rows, rows, P("fsdp", None), P("fsdp", None), rows),
        out_specs=(rows, rows, rows, P("replica", "fsdp"), P("fsdp", None), P("fsdp", None)),
        check_vma=False,
    )
```
